32 devices in a mesh: groups: 2 (over y), shard: 16 (over z, x, core).
Axes of the slice: x: 2, y: 2, z: 4, core: 2. Of those that a mesh axis runs over, the one named last changes fastest.
Arguments:
- traces: float32 [20736, 2048], P(('groups', 'shard')), parts along dimension 0, may hold values from -250 to 250
- cable_depth: float32 [32], P(('groups', 'shard')), parts along dimension 0, may hold values from 6 to 25
- receiver: int32 [20736], P(('groups', 'shard')), parts along dimension 0, may hold values from 0 to 671, as said below
- shot_slot: int32 [32], P('groups'), parts along dimension 0, may hold values from 0 to 15, as said below
- gather_home: int32 [1344], P('groups'), parts along dimension 0, may hold values from 0 to 671, each once
Outputs:
- filtered_gathers: float32 [1344, 16, 2048], P(('groups', 'shard')), parts along dimension 0
The draws below stay inside these ranges and needn't reach their ends.
There are 2 independent parts, one for each index of `groups`. The reference program is written for one: setup_inputs(seed, part) draws one part's arguments, and reference() takes and returns one part's arrays. A program takes and returns all parts, laid end to end along the dimension named above; each array names one. Nothing has to cross between parts.
Inputs may be any that keep to these rules, and one draw needn't show every extreme that they name: The 648 receiver bins of one record are distinct. `shot_slot`: every record has a position of its own.
All inputs are finite; a program needn't handle non-finite values.
Results may differ from the reference program's by a relative error of at most 0.0081.
Values may be sent and summed in bfloat16 or wider, within the bound.
A program may use at most 64 MiB of HBM per device.

```python
import math
import jax
import jax.numpy as jnp
from jax import lax

NT = 2048
NCH = 648
FREQ = 576
RECORDS = 16
TRACES = 10368
NREC = 672


def slot_order(key):
    return jax.random.permutation(jax.random.fold_in(key, 17), RECORDS).astype(jnp.int32)


def draw_shot_slot(key, part):
    return slot_order(key)


def draw_receiver(key, part):
    slots = slot_order(key)
    room = NREC - NCH - RECORDS + 1
    skips = jax.random.randint(jax.random.fold_in(key, 23), (RECORDS, NCH), 0, 2).astype(jnp.int32)
    skipped = jnp.cumsum(skips, axis=1) - skips
    channels = jnp.arange(NCH, dtype=jnp.int32)
    bins = slots[:, None] + channels[None, :] + jnp.minimum(skipped, room)
    bins = jnp.where(channels[None, :] == NCH - 1, slots[:, None] + NCH - 1 + room, bins)
    return bins.reshape(TRACES).astype(jnp.int32)


def draw_traces(key, part):
    record_index = (jnp.arange(TRACES, dtype=jnp.int32) // NCH).astype(jnp.float32)
    ramp = jnp.exp(0.5 * math.log(3.0) * record_index / max(RECORDS - 1, 1))
    sample_index = jnp.arange(NT, dtype=jnp.float32) / NT
    noise = jnp.clip(jax.random.normal(jax.random.fold_in(key, 31), (TRACES, NT), jnp.float32), -6.0, 6.0)
    decay = jnp.exp(-math.log(10.0) * sample_index)
    trace_scale = jnp.exp(jax.random.uniform(jax.random.fold_in(key, 41), (TRACES,), jnp.float32, 0.0, math.log(10.0)))
    return (noise * (ramp * trace_scale)[:, None] * decay[None, :]).astype(jnp.float32)


def block_scale(rng, extent, cuts, smallest, largest):
    def one(dim, blocks):
        heights = jax.random.uniform(jax.random.fold_in(jax.random.fold_in(rng, 6), dim), (blocks,), jnp.float32, smallest / len(cuts), largest / len(cuts))
        return jnp.repeat(jnp.exp(heights), extent[dim] // blocks).reshape((-1,) + (1,) * (len(extent) - dim - 1))

    factor_of = one(*cuts[0])
    for cut in cuts[1:]:
        factor_of = factor_of * one(*cut)
    return factor_of


def setup_inputs(seed: int = 0, part: int = 0) -> dict:
    streams_of = jax.random.split(jax.random.key(seed), 6)
    part_keys = jax.random.split(jax.random.fold_in(streams_of[5], part), 6)
    return {
        "traces": draw_traces(jax.random.fold_in(jax.random.fold_in(streams_of[5], part), 71), part),
        "cable_depth": jnp.clip(6.0 + 19.0 * jax.random.uniform(part_keys[1], (RECORDS,), jnp.float32) ** block_scale(part_keys[1], (RECORDS,), ((0, 16),), -0.2, 0.2), 6.0, 25.0),
        "receiver": draw_receiver(jax.random.fold_in(jax.random.fold_in(streams_of[5], part), 71), part),
        "shot_slot": draw_shot_slot(jax.random.fold_in(jax.random.fold_in(streams_of[5], part), 71), part),
        "gather_home": jax.random.permutation(part_keys[4], NREC).astype(jnp.int32),
    }


sample_step = 0.002
water_speed = 1500.0
channel_spacing = 12.5
shot_spacing = 25.0
surface_reflect = 0.9
ghost_floor = 0.1
reject_speed = 1500.0
low_floor = 4.0 * math.pi
energy_eps = 1e-06

def forward_time(n_samples, first_bin, band_size):
    samples = jnp.arange(n_samples, dtype=jnp.int32)
    freq_bins = first_bin + jnp.arange(band_size, dtype=jnp.int32)
    angles = (samples[:, None] * freq_bins[None, :] % n_samples).astype(jnp.float32) * (2.0 * math.pi / n_samples)
    return jnp.concatenate([jnp.cos(angles), -jnp.sin(angles)], axis=1).astype(jnp.bfloat16)

def inverse_time(n_samples, first_bin, band_size):
    samples = jnp.arange(n_samples, dtype=jnp.int32)
    freq_bins = first_bin + jnp.arange(band_size, dtype=jnp.int32)
    angles = (freq_bins[:, None] * samples[None, :] % n_samples).astype(jnp.float32) * (2.0 * math.pi / n_samples)
    weights = jnp.where(freq_bins == 0, 1.0, 2.0).astype(jnp.float32)[:, None]
    return jnp.concatenate([weights * jnp.cos(angles), -weights * jnp.sin(angles)], axis=0).astype(jnp.bfloat16)

def wave_tables(n_channels):
    wave_index = jnp.arange(n_channels, dtype=jnp.int32)
    angles = (wave_index[:, None] * wave_index[None, :] % n_channels).astype(jnp.float32) * (2.0 * math.pi / n_channels)
    return (jnp.cos(angles).astype(jnp.bfloat16), jnp.sin(angles).astype(jnp.bfloat16))

def angular_band(n_samples, first_bin, band_size):
    freq_bins = (first_bin + jnp.arange(band_size, dtype=jnp.int32)).astype(jnp.float32)
    return 2.0 * math.pi * freq_bins / (n_samples * sample_step)

def ghost_operator(n_channels, n_samples, first_bin, band_size, depth_value):
    angular = angular_band(n_samples, first_bin, band_size)
    wave_index = jnp.arange(n_channels, dtype=jnp.int32)
    signed = jnp.where(wave_index <= n_channels // 2, wave_index, wave_index - n_channels).astype(jnp.float32)
    wave_number = 2.0 * math.pi * signed / (n_channels * channel_spacing)
    slowness = angular / water_speed
    vertical = jnp.sqrt(jnp.maximum(slowness[None, :] * slowness[None, :] - wave_number[:, None] * wave_number[:, None], 0.0))
    angles = 2.0 * vertical * depth_value
    cosine = jnp.cos(angles)
    denominator = 1.0 - 2.0 * surface_reflect * cosine + surface_reflect * surface_reflect + ghost_floor
    return ((1.0 - surface_reflect * cosine) / denominator, -surface_reflect * jnp.sin(angles) / denominator)

def deghost(record, depth_value, first_bin, band_size):
    n_channels, n_samples = record.shape
    spectra = jnp.dot(record.astype(jnp.bfloat16), forward_time(n_samples, first_bin, band_size), preferred_element_type=jnp.float32).astype(jnp.bfloat16)
    cos_wave, sin_wave = wave_tables(n_channels)
    plain = jnp.dot(cos_wave, spectra, preferred_element_type=jnp.float32)
    turned = jnp.dot(sin_wave, spectra, preferred_element_type=jnp.float32)
    wave_re = plain[:, :band_size] + turned[:, band_size:]
    wave_im = plain[:, band_size:] - turned[:, :band_size]
    gain_re, gain_im = ghost_operator(n_channels, n_samples, first_bin, band_size, depth_value)
    lifted = jnp.concatenate([gain_re * wave_re - gain_im * wave_im, gain_re * wave_im + gain_im * wave_re], axis=1).astype(jnp.bfloat16)
    plain = jnp.dot(cos_wave, lifted, preferred_element_type=jnp.float32)
    turned = jnp.dot(sin_wave, lifted, preferred_element_type=jnp.float32)
    back_re = (plain[:, :band_size] - turned[:, band_size:]) / n_channels
    back_im = (plain[:, band_size:] + turned[:, :band_size]) / n_channels
    cleaned = jnp.concatenate([back_re, back_im], axis=1)
    return (cleaned.astype(jnp.bfloat16), jnp.sum(cleaned * cleaned))

def shot_tables(positions, records):
    wave_index = jnp.arange(2 * records, dtype=jnp.int32)
    angles = (positions[:, None] * wave_index[None, :] % (2 * records)).astype(jnp.float32) * (math.pi / records)
    return (jnp.cos(angles).astype(jnp.bfloat16), jnp.sin(angles).astype(jnp.bfloat16))

def shot_filter(records, n_samples, first_bin, band_size):
    angular = angular_band(n_samples, first_bin, band_size)
    wave_index = jnp.arange(2 * records, dtype=jnp.int32)
    signed = jnp.where(wave_index <= records, wave_index, wave_index - 2 * records).astype(jnp.float32)
    shot_number = 2.0 * math.pi * signed / (2 * records * shot_spacing)
    reject_ratio = reject_speed * jnp.abs(shot_number)[:, None] / (angular[None, :] + low_floor)
    squared = reject_ratio * reject_ratio
    response = 1.0 / (1.0 + squared * squared) / (2.0 * records)
    return jnp.concatenate([response, response], axis=1)

def reference(traces, cable_depth, receiver, shot_slot, gather_home):
    records = cable_depth.shape[0]
    n_samples = traces.shape[1]
    stacked = traces.reshape(records, NCH, n_samples)

    def clean_one(item):
        record, depth_value = item
        return deghost(record, depth_value, 0, FREQ)
    clean_rows, energies = lax.map(clean_one, (stacked, cable_depth))
    total_energy = jnp.sum(energies)
    out_scale = 1.0 / jnp.sqrt(2.0 * FREQ * (total_energy / (TRACES * FREQ) + energy_eps))
    targets = jnp.take(gather_home, receiver, axis=0).astype(jnp.int32)
    positions = jnp.repeat(shot_slot, NCH).astype(jnp.int32)
    gathered = jnp.zeros((NREC, records, 2 * FREQ), jnp.bfloat16).at[targets, positions].set(clean_rows.reshape(TRACES, 2 * FREQ))
    cos_shot, sin_shot = shot_tables(jnp.arange(records, dtype=jnp.int32), records)
    response = shot_filter(records, n_samples, 0, FREQ)
    inverse = inverse_time(n_samples, 0, FREQ)

    def filter_one(gather):
        even_part = (jnp.dot(cos_shot.T, gather, preferred_element_type=jnp.float32) * response).astype(jnp.bfloat16)
        odd_part = (jnp.dot(sin_shot.T, gather, preferred_element_type=jnp.float32) * response).astype(jnp.bfloat16)
        filtered = (jnp.dot(cos_shot, even_part, preferred_element_type=jnp.float32) + jnp.dot(sin_shot, odd_part, preferred_element_type=jnp.float32)).astype(jnp.bfloat16)
        return jnp.dot(filtered, inverse, preferred_element_type=jnp.float32) * out_scale
    return lax.map(filter_one, gathered)
```

```python
import functools
import math

import jax
import jax.numpy as jnp
import ml_dtypes
import numpy as np
from jax import lax
from jax.experimental import pallas as pl
from jax.experimental.pallas import tpu as pltpu
from jax.sharding import PartitionSpec as P

FREQ = 576


sample_step = 0.002
water_speed = 1500.0
channel_spacing = 12.5
shot_spacing = 25.0
surface_reflect = 0.9
ghost_floor = 0.1
reject_speed = 1500.0
low_floor = 4.0 * math.pi
energy_eps = 1e-06


def forward_time(n_samples, first_bin, band_size):
    samples = jnp.arange(n_samples, dtype=jnp.int32)
    freq_bins = first_bin + jnp.arange(band_size, dtype=jnp.int32)
    angles = (samples[:, None] * freq_bins[None, :] % n_samples).astype(jnp.float32) * (
        2.0 * math.pi / n_samples
    )
    return jnp.concatenate([jnp.cos(angles), -jnp.sin(angles)], axis=1).astype(jnp.bfloat16)


def inverse_time(n_samples, first_bin, band_size):
    samples = jnp.arange(n_samples, dtype=jnp.int32)
    freq_bins = first_bin + jnp.arange(band_size, dtype=jnp.int32)
    angles = (freq_bins[:, None] * samples[None, :] % n_samples).astype(jnp.float32) * (
        2.0 * math.pi / n_samples
    )
    weights = jnp.where(freq_bins == 0, 1.0, 2.0).astype(jnp.float32)[:, None]
    return jnp.concatenate([weights * jnp.cos(angles), -weights * jnp.sin(angles)], axis=0).astype(
        jnp.bfloat16
    )


def wave_tables(n_channels):
    wave_index = jnp.arange(n_channels, dtype=jnp.int32)
    angles = (wave_index[:, None] * wave_index[None, :] % n_channels).astype(jnp.float32) * (
        2.0 * math.pi / n_channels
    )
    return (jnp.cos(angles).astype(jnp.bfloat16), jnp.sin(angles).astype(jnp.bfloat16))


def angular_band(n_samples, first_bin, band_size):
    freq_bins = (first_bin + jnp.arange(band_size, dtype=jnp.int32)).astype(jnp.float32)
    return 2.0 * math.pi * freq_bins / (n_samples * sample_step)


def ghost_operator(n_channels, n_samples, first_bin, band_size, depth_value):
    angular = angular_band(n_samples, first_bin, band_size)
    wave_index = jnp.arange(n_channels, dtype=jnp.int32)
    signed = jnp.where(wave_index <= n_channels // 2, wave_index, wave_index - n_channels).astype(
        jnp.float32
    )
    wave_number = 2.0 * math.pi * signed / (n_channels * channel_spacing)
    slowness = angular / water_speed
    vertical = jnp.sqrt(
        jnp.maximum(
            slowness[None, :] * slowness[None, :] - wave_number[:, None] * wave_number[:, None], 0.0
        )
    )
    angles = 2.0 * vertical * depth_value
    cosine = jnp.cos(angles)
    denominator = (
        1.0 - 2.0 * surface_reflect * cosine + surface_reflect * surface_reflect + ghost_floor
    )
    return (
        (1.0 - surface_reflect * cosine) / denominator,
        -surface_reflect * jnp.sin(angles) / denominator,
    )


def deghost(record, depth_value, first_bin, band_size):
    n_channels, n_samples = record.shape
    spectra = jnp.dot(
        record.astype(jnp.bfloat16),
        forward_time(n_samples, first_bin, band_size),
        preferred_element_type=jnp.float32,
    ).astype(jnp.bfloat16)
    cos_wave, sin_wave = wave_tables(n_channels)
    plain = jnp.dot(cos_wave, spectra, preferred_element_type=jnp.float32)
    turned = jnp.dot(sin_wave, spectra, preferred_element_type=jnp.float32)
    wave_re = plain[:, :band_size] + turned[:, band_size:]
    wave_im = plain[:, band_size:] - turned[:, :band_size]
    gain_re, gain_im = ghost_operator(n_channels, n_samples, first_bin, band_size, depth_value)
    lifted = jnp.concatenate(
        [gain_re * wave_re - gain_im * wave_im, gain_re * wave_im + gain_im * wave_re], axis=1
    ).astype(jnp.bfloat16)
    plain = jnp.dot(cos_wave, lifted, preferred_element_type=jnp.float32)
    turned = jnp.dot(sin_wave, lifted, preferred_element_type=jnp.float32)
    back_re = (plain[:, :band_size] - turned[:, band_size:]) / n_channels
    back_im = (plain[:, band_size:] + turned[:, :band_size]) / n_channels
    cleaned = jnp.concatenate([back_re, back_im], axis=1)
    return (cleaned.astype(jnp.bfloat16), jnp.sum(cleaned * cleaned))


def shot_tables(positions, records):
    wave_index = jnp.arange(2 * records, dtype=jnp.int32)
    angles = (positions[:, None] * wave_index[None, :] % (2 * records)).astype(jnp.float32) * (
        math.pi / records
    )
    return (jnp.cos(angles).astype(jnp.bfloat16), jnp.sin(angles).astype(jnp.bfloat16))


def shot_filter(records, n_samples, first_bin, band_size):
    angular = angular_band(n_samples, first_bin, band_size)
    wave_index = jnp.arange(2 * records, dtype=jnp.int32)
    signed = jnp.where(wave_index <= records, wave_index, wave_index - 2 * records).astype(
        jnp.float32
    )
    shot_number = 2.0 * math.pi * signed / (2 * records * shot_spacing)
    reject_ratio = reject_speed * jnp.abs(shot_number)[:, None] / (angular[None, :] + low_floor)
    squared = reject_ratio * reject_ratio
    response = 1.0 / (1.0 + squared * squared) / (2.0 * records)
    return jnp.concatenate([response, response], axis=1)


def place_rows(clean_rows, receiver, gather_home, records, per_device):
    targets = jnp.take(gather_home, receiver, axis=0)
    buffer = (
        jnp.zeros((records * per_device, clean_rows.shape[1]), jnp.bfloat16)
        .at[targets]
        .set(clean_rows)
    )
    return buffer.reshape(records, per_device, clean_rows.shape[1])


def filter_gathers(arrived, shot_slot, n_samples, first_bin, band_size):
    records = arrived.shape[0]
    cos_source, sin_source = shot_tables(shot_slot, records)
    cos_shot, sin_shot = shot_tables(jnp.arange(records, dtype=jnp.int32), records)
    response = shot_filter(records, n_samples, first_bin, band_size)[:, None, :]
    even_part = (
        jnp.einsum("sgf,sk->kgf", arrived, cos_source, preferred_element_type=jnp.float32)
        * response
    ).astype(jnp.bfloat16)
    odd_part = (
        jnp.einsum("sgf,sk->kgf", arrived, sin_source, preferred_element_type=jnp.float32)
        * response
    ).astype(jnp.bfloat16)
    filtered = (
        jnp.einsum("pk,kgf->gpf", cos_shot, even_part, preferred_element_type=jnp.float32)
        + jnp.einsum("pk,kgf->gpf", sin_shot, odd_part, preferred_element_type=jnp.float32)
    ).astype(jnp.bfloat16)
    return jnp.einsum(
        "gpf,ft->gpt",
        filtered,
        inverse_time(n_samples, first_bin, band_size),
        preferred_element_type=jnp.float32,
    )


def shards(traces, cable_depth, receiver, shot_slot, gather_home):
    records = lax.axis_size("shard")
    per_device = gather_home.shape[0] // records
    n_channels, n_samples = traces.shape
    clean_rows, energy = deghost(traces, cable_depth[0], 0, FREQ)
    outgoing = place_rows(clean_rows, receiver, gather_home, records, per_device)
    arrived = lax.all_to_all(outgoing, "shard", split_axis=0, concat_axis=0, tiled=True)
    summed = filter_gathers(arrived, shot_slot, n_samples, 0, FREQ)
    total_energy = lax.psum(energy, "shard")
    out_scale = 1.0 / jnp.sqrt(
        2.0 * FREQ * (total_energy / (n_channels * records * FREQ) + energy_eps)
    )
    return summed * out_scale


def round_up(value, unit):
    return -(-value // unit) * unit


LANES = 128
HALF = LANES // 2
GROUP = 3


def fused_tables(n_channels, n_samples, records, per_device):
    bf16 = ml_dtypes.bfloat16
    blocks = FREQ // HALF
    bins = np.arange(FREQ).reshape(blocks, HALF)
    samples = np.arange(n_samples)
    turn = 2.0 * np.pi / n_samples
    angle = (samples[:, None] * np.arange(FREQ)[None, :] % n_samples) * turn
    cos_t = np.cos(angle).reshape(n_samples, blocks, 1, HALF)
    sin_t = np.sin(angle).reshape(n_samples, blocks, 1, HALF)
    forward = np.concatenate([cos_t, -sin_t], axis=2).reshape(n_samples, blocks * LANES)
    weight = np.where(bins == 0, 1.0, 2.0)[None, :, None, :]
    inverse = np.concatenate([weight * cos_t, -weight * sin_t], axis=2)
    inverse = inverse.reshape(n_samples, blocks * LANES).T
    chunks = blocks // GROUP
    forward = forward.reshape(n_samples, chunks, GROUP * LANES).transpose(1, 0, 2)

    half_rows = round_up(n_channels // 2 + 1, 16)
    wave = np.zeros((2 * half_rows, 2 * half_rows))
    index = np.arange(n_channels // 2 + 1)
    angle = (index[:, None] * np.arange(n_channels)[None, :] % n_channels) * (
        2.0 * np.pi / n_channels
    )
    wave[: index.size, :n_channels] = np.cos(angle)
    wave[half_rows : half_rows + index.size, :n_channels] = np.sin(angle)
    own_mirror = (index * 2) % n_channels == 0
    wave[half_rows : half_rows + index.size][own_mirror] = 0.0
    twice = np.ones((2 * half_rows, 1))
    twice[: index.size, 0] = np.where(own_mirror, 1.0, 2.0)
    twice[half_rows : half_rows + index.size, 0] = 2.0
    wave = wave.astype(bf16)
    back = (wave.astype(np.float64) * twice).T.astype(bf16)

    angular = 2.0 * np.pi * np.arange(FREQ) / (n_samples * sample_step)
    number = 2.0 * np.pi * np.arange(half_rows) / (n_channels * channel_spacing)
    vertical = np.sqrt(
        np.maximum((angular / water_speed)[None, :] ** 2 - number[:, None] ** 2, 0.0)
    )
    vertical = (vertical / np.pi).reshape(half_rows, blocks, 1, HALF)
    vertical = np.concatenate([vertical, vertical], axis=2).reshape(half_rows, blocks * LANES)

    shots = np.arange(2 * records)
    signed = np.where(shots <= records, shots, shots - 2 * records)
    shot_number = 2.0 * np.pi * signed / (2 * records * shot_spacing)
    ratio = reject_speed * np.abs(shot_number)[:, None] / (angular[None, :] + low_floor)
    response = 1.0 / (1.0 + ratio**4) / (2.0 * records)
    apart = np.arange(records)
    lag = np.cos(np.pi / records * (apart[:, None] * shots[None, :] % (2 * records))) @ response
    lag = lag.reshape(records, chunks, GROUP, 1, HALF)
    lag = np.broadcast_to(lag, (records, chunks, GROUP, 2, HALF)).reshape(
        records, chunks, GROUP, 1, LANES
    )
    packed = round_up(GROUP * per_device, 16)
    taps = np.zeros((chunks, records, packed, LANES))
    taps[:, :, : GROUP * per_device] = (
        np.broadcast_to(lag, (records, chunks, GROUP, per_device, LANES))
        .transpose(1, 0, 2, 3, 4)
        .reshape(chunks, records, GROUP * per_device, LANES)
    )
    return (
        forward.astype(bf16),
        inverse.astype(bf16),
        wave,
        back,
        vertical.astype(np.float32),
        taps.astype(np.float32),
    )


SINE = [(-1.0) ** i * (2.0 * math.pi) ** (2 * i + 1) / math.factorial(2 * i + 1) for i in range(6)]


def gain_tiles(vertical, depth, n_channels):
    left = lax.broadcasted_iota(jnp.int32, vertical.shape, 1) < HALF
    turns = vertical * depth - jnp.where(left, 0.25, 0.0)
    offset = 0.25 - jnp.abs(turns - jnp.floor(turns + 0.5))
    square = offset * offset
    value = jnp.full_like(square, SINE[-1])
    for coefficient in SINE[-2::-1]:
        value = value * square + coefficient
    value = value * offset
    swapped = pltpu.roll(value, HALF, 1)
    cosine = jnp.where(left, swapped, value)
    sine = jnp.where(left, value, -swapped)
    denominator = (
        1.0 - 2.0 * surface_reflect * cosine + surface_reflect * surface_reflect + ghost_floor
    )
    scale = 1.0 / (denominator * n_channels)
    return (1.0 - surface_reflect * cosine) * scale, surface_reflect * sine * scale


def exchange_kernel(
    records,
    per_device,
    chunks,
    traces,
    forward,
    wave,
    back,
    vertical,
    taps,
    depth,
    order,
    home,
    receiver,
    filtered,
    energy,
    raw,
    rounded,
    table,
    lag,
    placed,
    spectra,
    lifted,
    packed,
    shots,
    ordered,
    sums,
    load_sem,
    send_sem,
    recv_sem,
    sum_send,
    sum_recv,
    *slots,
):
    outgoing, arrived = slots[:chunks], slots[chunks:]
    me = lax.axis_index("shard")
    n_channels, n_samples = raw.shape
    padded = rounded.shape[0]
    half_rows = padded // 2
    home_rows = placed.shape[0]
    stride = home_rows // records

    def partner(step):
        if records & (records - 1):
            return lax.rem(me + step, records)
        other = me
        bit = 1
        while bit < records:
            if step & bit:
                other = other + bit * (1 - 2 * lax.rem(me // bit, 2))
            bit *= 2
        return other

    steps = [s for s in range(records - 1, 0, -1)]

    copies = [pltpu.make_async_copy(traces, raw, load_sem.at[0])]
    for c in range(chunks):
        copies.append(pltpu.make_async_copy(forward.at[c], table.at[c], load_sem.at[1 + 2 * c]))
        copies.append(pltpu.make_async_copy(taps.at[c], lag.at[c], load_sem.at[2 + 2 * c]))
    for copy in copies[:2]:
        copy.start()

    barrier = pltpu.get_barrier_semaphore()
    for step in steps:
        pl.semaphore_signal(
            barrier,
            inc=1,
            device_id={"shard": partner(step)},
            device_id_type=pl.DeviceIdType.MESH,
        )

    bins = lax.broadcasted_iota(jnp.int32, (home.shape[1], padded), 0)
    chosen = (bins == receiver[...]).astype(jnp.bfloat16)
    by_bin = jnp.dot(chosen, back[...], preferred_element_type=jnp.float32).astype(jnp.bfloat16)
    rows = lax.broadcasted_iota(jnp.int32, (home_rows, home.shape[1]), 0)
    chosen = (rows == home[...]).astype(jnp.bfloat16)
    placed[...] = jnp.dot(chosen, by_bin, preferred_element_type=jnp.float32).astype(jnp.bfloat16)
    packed[...] = jnp.zeros_like(packed)
    rounded[...] = jnp.zeros_like(rounded)

    copies[0].wait()
    for copy in copies[2:]:
        copy.start()
    rounded[:n_channels, :] = raw[...].astype(jnp.bfloat16)

    total = jnp.zeros((8, LANES), jnp.float32)
    sends = []
    for c in range(chunks):
        copies[1 + 2 * c].wait()
        spectra[...] = jnp.dot(
            rounded[...], table[c], preferred_element_type=jnp.float32
        ).astype(jnp.bfloat16)
        turned = jnp.dot(wave[...], spectra[...], preferred_element_type=jnp.float32)
        for b in range(GROUP):
            lanes = slice(b * LANES, (b + 1) * LANES)
            column = c * GROUP + b
            straight, crossed = gain_tiles(
                vertical[:, column * LANES : (column + 1) * LANES], depth[0], n_channels
            )
            for part in range(2):
                part_rows = slice(part * half_rows, (part + 1) * half_rows)
                value = turned[part_rows, lanes]
                lifted[part_rows, lanes] = (
                    straight * value + crossed * pltpu.roll(value, HALF, 1)
                ).astype(jnp.bfloat16)
        cleaned = jnp.dot(placed[...], lifted[...], preferred_element_type=jnp.float32)
        for b in range(GROUP):
            block = cleaned[:, b * LANES : (b + 1) * LANES]
            total = total + jnp.sum((block * block).reshape(-1, 8, LANES), axis=0)
            for d in range(records):
                packed[d, b * per_device : (b + 1) * per_device, :] = block[
                    d * stride : d * stride + per_device
                ]
        outgoing[c][...] = packed[...].astype(jnp.bfloat16)
        if c == 0:
            pl.semaphore_wait(barrier, records - 1)
        for i, step in enumerate(steps):
            other = partner(step)
            send = pltpu.make_async_remote_copy(
                src_ref=outgoing[c].at[other],
                dst_ref=arrived[c].at[me],
                send_sem=send_sem.at[c, i],
                recv_sem=recv_sem.at[c, i],
                device_id={"shard": other},
                device_id_type=pl.DeviceIdType.MESH,
            )
            send.start()
            sends.append(send)
        arrived[c][me] = outgoing[c][me]

    sums[me] = total
    for i, step in enumerate(steps):
        send = pltpu.make_async_remote_copy(
            src_ref=sums.at[me],
            dst_ref=sums.at[me],
            send_sem=sum_send.at[i],
            recv_sem=sum_recv.at[i],
            device_id={"shard": partner(step)},
            device_id_type=pl.DeviceIdType.MESH,
        )
        send.start()
        sends.append(send)

    tile = 16
    for c in range(chunks):
        copies[2 + 2 * c].wait()
        for send in sends[c * len(steps) : (c + 1) * len(steps)]:
            send.wait()

        def filter_rows(r, carry):
            at = pl.ds(pl.multiple_of(r * tile, tile), tile)
            values = [arrived[c][order[q], at, :].astype(jnp.float32) for q in range(records)]
            for p in range(records):
                result = None
                for q in range(records):
                    term = lag[c, abs(p - q), at, :] * values[q]
                    result = term if result is None else result + term
                shots[p, at, :] = result
            return carry

        lax.fori_loop(0, shots.shape[1] // tile, filter_rows, 0)
        for b in range(GROUP):
            for p in range(records):
                ordered[b, pl.ds(p, per_device, stride=records), :] = shots[
                    p, b * per_device : (b + 1) * per_device, :
                ]
            column = c * GROUP + b
            filtered[:, column * LANES : (column + 1) * LANES] = ordered[b].astype(jnp.bfloat16)
    for send in sends[chunks * len(steps) :]:
        send.wait()
    energy[...] = jnp.sum(sums[...], axis=0)


def exchange(traces, cable_depth, receiver, shot_slot, gather_home, tables, records):
    forward, _, wave, back, vertical, taps = tables
    n_channels, n_samples = traces.shape
    n_bins = gather_home.shape[0]
    per_device = n_bins // records
    chunks, _, packed_rows, _ = taps.shape
    stride = round_up(per_device, 16)
    padded = wave.shape[0]
    order = jnp.sum(
        jnp.where(
            shot_slot[None, :] == jnp.arange(records, dtype=jnp.int32)[:, None],
            jnp.arange(records, dtype=jnp.int32)[None, :],
            0,
        ),
        axis=1,
    )
    home = (gather_home // per_device * stride + gather_home % per_device)[None, :]
    channels = jnp.pad(receiver, (0, padded - n_channels), constant_values=-1)[None, :]
    vmem = pl.BlockSpec(memory_space=pltpu.VMEM)
    smem = pl.BlockSpec(memory_space=pltpu.SMEM)
    anywhere = pl.BlockSpec(memory_space=pl.ANY)
    width = GROUP * LANES
    peers = records - 1
    slot = pltpu.VMEM((records, packed_rows, LANES), jnp.bfloat16)
    return pl.pallas_call(
        functools.partial(exchange_kernel, records, per_device, chunks),
        out_shape=(
            jax.ShapeDtypeStruct((per_device * records, chunks * width), jnp.bfloat16),
            jax.ShapeDtypeStruct((8, LANES), jnp.float32),
        ),
        in_specs=[anywhere, anywhere, vmem, vmem, vmem, anywhere, smem, smem, vmem, vmem],
        out_specs=(vmem, vmem),
        scratch_shapes=[
            pltpu.VMEM((n_channels, n_samples), jnp.float32),
            pltpu.VMEM((padded, n_samples), jnp.bfloat16),
            pltpu.VMEM(forward.shape, jnp.bfloat16),
            pltpu.VMEM(taps.shape, jnp.float32),
            pltpu.VMEM((records * stride, padded), jnp.bfloat16),
            pltpu.VMEM((padded, width), jnp.bfloat16),
            pltpu.VMEM((padded, width), jnp.bfloat16),
            pltpu.VMEM((records, packed_rows, LANES), jnp.float32),
            pltpu.VMEM((records, packed_rows, LANES), jnp.float32),
            pltpu.VMEM((GROUP, per_device * records, LANES), jnp.float32),
            pltpu.VMEM((records, 8, LANES), jnp.float32),
            pltpu.SemaphoreType.DMA((1 + 2 * chunks,)),
            pltpu.SemaphoreType.DMA((chunks, peers)),
            pltpu.SemaphoreType.DMA((chunks, peers)),
            pltpu.SemaphoreType.DMA((peers,)),
            pltpu.SemaphoreType.DMA((peers,)),
        ]
        + [slot] * (2 * chunks),
        compiler_params=pltpu.CompilerParams(
            collective_id=0, has_side_effects=True, vmem_limit_bytes=56 * 1024 * 1024
        ),
    )(traces, forward, wave, back, vertical, taps, cable_depth, order, home, channels)


def inverse_kernel(count, energy, filtered, inverse, out):
    total = jnp.sum(energy[...])
    scale = lax.rsqrt(jnp.full((1, 1), 2.0 * FREQ, jnp.float32) * (total / count + energy_eps))
    out[...] = (
        jnp.dot(filtered[...], inverse[...], preferred_element_type=jnp.float32) * scale
    )


def invert(filtered, energy, inverse, count):
    n_rows, depth = filtered.shape
    n_samples = inverse.shape[1]
    block = 512
    return pl.pallas_call(
        functools.partial(inverse_kernel, count),
        out_shape=jax.ShapeDtypeStruct((n_rows, n_samples), jnp.float32),
        grid=(n_samples // block,),
        in_specs=[
            pl.BlockSpec((8, LANES), lambda i: (0, 0)),
            pl.BlockSpec((n_rows, depth), lambda i: (0, 0)),
            pl.BlockSpec((depth, block), lambda i: (0, i)),
        ],
        out_specs=pl.BlockSpec((n_rows, block), lambda i: (0, i)),
        compiler_params=pltpu.CompilerParams(vmem_limit_bytes=48 * 1024 * 1024),
    )(energy, filtered, inverse)


def fused_shards(traces, cable_depth, receiver, shot_slot, gather_home):
    records = lax.axis_size("shard")
    n_channels, n_samples = traces.shape
    per_device = gather_home.shape[0] // records
    tables = fused_tables(n_channels, n_samples, records, per_device)
    filtered, energy = exchange(
        traces, cable_depth, receiver, shot_slot, gather_home, tables, records
    )
    out = invert(filtered, energy, tables[1], float(n_channels * records * FREQ))
    return out.reshape(per_device, records, n_samples)


def solution(mesh):
    in_specs = (
        P(("groups", "shard"), None),
        P(("groups", "shard")),
        P(("groups", "shard")),
        P("groups"),
        P("groups"),
    )
    out_specs = P(("groups", "shard"), None, None)
    body = fused_shards if mesh.shape["shard"] <= 16 else shards
    return jax.shard_map(body, mesh=mesh, in_specs=in_specs, out_specs=out_specs, check_vma=False)
```

```python
import functools
import math

import jax
import jax.numpy as jnp
import ml_dtypes
import numpy as np
from jax import lax
from jax.experimental import pallas as pl
from jax.experimental.pallas import tpu as pltpu
from jax.sharding import PartitionSpec as P

FREQ = 576


sample_step = 0.002
water_speed = 1500.0
channel_spacing = 12.5
shot_spacing = 25.0
surface_reflect = 0.9
ghost_floor = 0.1
reject_speed = 1500.0
low_floor = 4.0 * math.pi
energy_eps = 1e-06


def forward_time(n_samples, first_bin, band_size):
    samples = jnp.arange(n_samples, dtype=jnp.int32)
    freq_bins = first_bin + jnp.arange(band_size, dtype=jnp.int32)
    angles = (samples[:, None] * freq_bins[None, :] % n_samples).astype(jnp.float32) * (
        2.0 * math.pi / n_samples
    )
    return jnp.concatenate([jnp.cos(angles), -jnp.sin(angles)], axis=1).astype(jnp.bfloat16)


def inverse_time(n_samples, first_bin, band_size):
    samples = jnp.arange(n_samples, dtype=jnp.int32)
    freq_bins = first_bin + jnp.arange(band_size, dtype=jnp.int32)
    angles = (freq_bins[:, None] * samples[None, :] % n_samples).astype(jnp.float32) * (
        2.0 * math.pi / n_samples
    )
    weights = jnp.where(freq_bins == 0, 1.0, 2.0).astype(jnp.float32)[:, None]
    return jnp.concatenate([weights * jnp.cos(angles), -weights * jnp.sin(angles)], axis=0).astype(
        jnp.bfloat16
    )


def wave_tables(n_channels):
    wave_index = jnp.arange(n_channels, dtype=jnp.int32)
    angles = (wave_index[:, None] * wave_index[None, :] % n_channels).astype(jnp.float32) * (
        2.0 * math.pi / n_channels
    )
    return (jnp.cos(angles).astype(jnp.bfloat16), jnp.sin(angles).astype(jnp.bfloat16))


def angular_band(n_samples, first_bin, band_size):
    freq_bins = (first_bin + jnp.arange(band_size, dtype=jnp.int32)).astype(jnp.float32)
    return 2.0 * math.pi * freq_bins / (n_samples * sample_step)


def ghost_operator(n_channels, n_samples, first_bin, band_size, depth_value):
    angular = angular_band(n_samples, first_bin, band_size)
    wave_index = jnp.arange(n_channels, dtype=jnp.int32)
    signed = jnp.where(wave_index <= n_channels // 2, wave_index, wave_index - n_channels).astype(
        jnp.float32
    )
    wave_number = 2.0 * math.pi * signed / (n_channels * channel_spacing)
    slowness = angular / water_speed
    vertical = jnp.sqrt(
        jnp.maximum(
            slowness[None, :] * slowness[None, :] - wave_number[:, None] * wave_number[:, None], 0.0
        )
    )
    angles = 2.0 * vertical * depth_value
    cosine = jnp.cos(angles)
    denominator = (
        1.0 - 2.0 * surface_reflect * cosine + surface_reflect * surface_reflect + ghost_floor
    )
    return (
        (1.0 - surface_reflect * cosine) / denominator,
        -surface_reflect * jnp.sin(angles) / denominator,
    )


def deghost(record, depth_value, first_bin, band_size):
    n_channels, n_samples = record.shape
    spectra = jnp.dot(
        record.astype(jnp.bfloat16),
        forward_time(n_samples, first_bin, band_size),
        preferred_element_type=jnp.float32,
    ).astype(jnp.bfloat16)
    cos_wave, sin_wave = wave_tables(n_channels)
    plain = jnp.dot(cos_wave, spectra, preferred_element_type=jnp.float32)
    turned = jnp.dot(sin_wave, spectra, preferred_element_type=jnp.float32)
    wave_re = plain[:, :band_size] + turned[:, band_size:]
    wave_im = plain[:, band_size:] - turned[:, :band_size]
    gain_re, gain_im = ghost_operator(n_channels, n_samples, first_bin, band_size, depth_value)
    lifted = jnp.concatenate(
        [gain_re * wave_re - gain_im * wave_im, gain_re * wave_im + gain_im * wave_re], axis=1
    ).astype(jnp.bfloat16)
    plain = jnp.dot(cos_wave, lifted, preferred_element_type=jnp.float32)
    turned = jnp.dot(sin_wave, lifted, preferred_element_type=jnp.float32)
    back_re = (plain[:, :band_size] - turned[:, band_size:]) / n_channels
    back_im = (plain[:, band_size:] + turned[:, :band_size]) / n_channels
    cleaned = jnp.concatenate([back_re, back_im], axis=1)
    return (cleaned.astype(jnp.bfloat16), jnp.sum(cleaned * cleaned))


def shot_tables(positions, records):
    wave_index = jnp.arange(2 * records, dtype=jnp.int32)
    angles = (positions[:, None] * wave_index[None, :] % (2 * records)).astype(jnp.float32) * (
        math.pi / records
    )
    return (jnp.cos(angles).astype(jnp.bfloat16), jnp.sin(angles).astype(jnp.bfloat16))


def shot_filter(records, n_samples, first_bin, band_size):
    angular = angular_band(n_samples, first_bin, band_size)
    wave_index = jnp.arange(2 * records, dtype=jnp.int32)
    signed = jnp.where(wave_index <= records, wave_index, wave_index - 2 * records).astype(
        jnp.float32
    )
    shot_number = 2.0 * math.pi * signed / (2 * records * shot_spacing)
    reject_ratio = reject_speed * jnp.abs(shot_number)[:, None] / (angular[None, :] + low_floor)
    squared = reject_ratio * reject_ratio
    response = 1.0 / (1.0 + squared * squared) / (2.0 * records)
    return jnp.concatenate([response, response], axis=1)


def place_rows(clean_rows, receiver, gather_home, records, per_device):
    targets = jnp.take(gather_home, receiver, axis=0)
    buffer = (
        jnp.zeros((records * per_device, clean_rows.shape[1]), jnp.bfloat16)
        .at[targets]
        .set(clean_rows)
    )
    return buffer.reshape(records, per_device, clean_rows.shape[1])


def filter_gathers(arrived, shot_slot, n_samples, first_bin, band_size):
    records = arrived.shape[0]
    cos_source, sin_source = shot_tables(shot_slot, records)
    cos_shot, sin_shot = shot_tables(jnp.arange(records, dtype=jnp.int32), records)
    response = shot_filter(records, n_samples, first_bin, band_size)[:, None, :]
    even_part = (
        jnp.einsum("sgf,sk->kgf", arrived, cos_source, preferred_element_type=jnp.float32)
        * response
    ).astype(jnp.bfloat16)
    odd_part = (
        jnp.einsum("sgf,sk->kgf", arrived, sin_source, preferred_element_type=jnp.float32)
        * response
    ).astype(jnp.bfloat16)
    filtered = (
        jnp.einsum("pk,kgf->gpf", cos_shot, even_part, preferred_element_type=jnp.float32)
        + jnp.einsum("pk,kgf->gpf", sin_shot, odd_part, preferred_element_type=jnp.float32)
    ).astype(jnp.bfloat16)
    return jnp.einsum(
        "gpf,ft->gpt",
        filtered,
        inverse_time(n_samples, first_bin, band_size),
        preferred_element_type=jnp.float32,
    )


def shards(traces, cable_depth, receiver, shot_slot, gather_home):
    records = lax.axis_size("shard")
    per_device = gather_home.shape[0] // records
    n_channels, n_samples = traces.shape
    clean_rows, energy = deghost(traces, cable_depth[0], 0, FREQ)
    outgoing = place_rows(clean_rows, receiver, gather_home, records, per_device)
    arrived = lax.all_to_all(outgoing, "shard", split_axis=0, concat_axis=0, tiled=True)
    summed = filter_gathers(arrived, shot_slot, n_samples, 0, FREQ)
    total_energy = lax.psum(energy, "shard")
    out_scale = 1.0 / jnp.sqrt(
        2.0 * FREQ * (total_energy / (n_channels * records * FREQ) + energy_eps)
    )
    return summed * out_scale


def round_up(value, unit):
    return -(-value // unit) * unit


LANES = 128
HALF = LANES // 2
GROUPS = (1, 3, 3, 2)


def fused_tables(n_channels, n_samples, records, per_device):
    bf16 = ml_dtypes.bfloat16
    blocks = FREQ // HALF
    bins = np.arange(FREQ).reshape(blocks, HALF)
    samples = np.arange(n_samples)
    turn = 2.0 * np.pi / n_samples
    angle = (samples[:, None] * np.arange(FREQ)[None, :] % n_samples) * turn
    cos_t = np.cos(angle).reshape(n_samples, blocks, 1, HALF)
    sin_t = np.sin(angle).reshape(n_samples, blocks, 1, HALF)
    forward = np.concatenate([cos_t, -sin_t], axis=2).reshape(n_samples, blocks * LANES)
    weight = np.where(bins == 0, 1.0, 2.0)[None, :, None, :]
    inverse = np.concatenate([weight * cos_t, -weight * sin_t], axis=2)
    inverse = inverse.reshape(n_samples, blocks * LANES).T
    half_rows = round_up(n_channels // 2 + 1, 16)
    wave = np.zeros((2 * half_rows, 2 * half_rows))
    index = np.arange(n_channels // 2 + 1)
    angle = (index[:, None] * np.arange(n_channels)[None, :] % n_channels) * (
        2.0 * np.pi / n_channels
    )
    wave[: index.size, :n_channels] = np.cos(angle)
    wave[half_rows : half_rows + index.size, :n_channels] = np.sin(angle)
    own_mirror = (index * 2) % n_channels == 0
    wave[half_rows : half_rows + index.size][own_mirror] = 0.0
    twice = np.ones((2 * half_rows, 1))
    twice[: index.size, 0] = np.where(own_mirror, 1.0, 2.0)
    twice[half_rows : half_rows + index.size, 0] = 2.0
    wave = wave.astype(bf16)
    back = (wave.astype(np.float64) * twice).T.astype(bf16)

    angular = 2.0 * np.pi * np.arange(FREQ) / (n_samples * sample_step)
    number = 2.0 * np.pi * np.arange(half_rows) / (n_channels * channel_spacing)
    vertical = np.sqrt(
        np.maximum((angular / water_speed)[None, :] ** 2 - number[:, None] ** 2, 0.0)
    )
    vertical = (vertical / np.pi).reshape(half_rows, blocks, 1, HALF)
    vertical = np.concatenate([vertical, vertical], axis=2).reshape(half_rows, blocks * LANES)

    shots = np.arange(2 * records)
    signed = np.where(shots <= records, shots, shots - 2 * records)
    shot_number = 2.0 * np.pi * signed / (2 * records * shot_spacing)
    ratio = reject_speed * np.abs(shot_number)[:, None] / (angular[None, :] + low_floor)
    response = 1.0 / (1.0 + ratio**4) / (2.0 * records)
    apart = np.arange(records)
    lag = np.cos(np.pi / records * (apart[:, None] * shots[None, :] % (2 * records))) @ response
    lag = lag.reshape(records, blocks, 1, HALF)
    lag = np.concatenate([lag, lag], axis=2).reshape(records, blocks, 1, LANES)
    lag = np.broadcast_to(lag, (records, blocks, per_device, LANES))
    taps = []
    first = 0
    for group in GROUPS:
        filled = group * per_device
        part = np.zeros((records, round_up(filled, 16), LANES))
        part[:, :filled] = lag[:, first : first + group].reshape(records, filled, LANES)
        taps.append(part)
        first += group
    taps = np.concatenate(taps, axis=1)
    return (
        forward.astype(bf16),
        inverse.astype(bf16),
        wave,
        back,
        vertical.astype(np.float32),
        taps.astype(np.float32),
    )


SINE = [(-1.0) ** i * (2.0 * math.pi) ** (2 * i + 1) / math.factorial(2 * i + 1) for i in range(6)]


def gain_tiles(vertical, depth, n_channels):
    left = lax.broadcasted_iota(jnp.int32, vertical.shape, 1) < HALF
    turns = vertical * depth - jnp.where(left, 0.25, 0.0)
    offset = 0.25 - jnp.abs(turns - jnp.floor(turns + 0.5))
    square = offset * offset
    value = jnp.full_like(square, SINE[-1])
    for coefficient in SINE[-2::-1]:
        value = value * square + coefficient
    value = value * offset
    swapped = pltpu.roll(value, HALF, 1)
    cosine = jnp.where(left, swapped, value)
    sine = jnp.where(left, value, -swapped)
    denominator = (
        1.0 - 2.0 * surface_reflect * cosine + surface_reflect * surface_reflect + ghost_floor
    )
    scale = 1.0 / (denominator * n_channels)
    return (1.0 - surface_reflect * cosine) * scale, surface_reflect * sine * scale


def exchange_kernel(
    records,
    per_device,
    stride,
    traces,
    forward,
    wave_table,
    back_table,
    vertical_table,
    taps,
    inverse_table,
    depth,
    shot_slot,
    home,
    receiver,
    last,
    energy,
    partial,
    raw,
    rounded,
    table,
    wave,
    back,
    vertical,
    lag,
    inverse,
    placed,
    spectra,
    lifted,
    packed,
    shots,
    ordered,
    filtered,
    summed,
    sums,
    load_sem,
    send_sem,
    recv_sem,
    sum_send,
    sum_recv,
    *slots,
):
    chunks = len(GROUPS)
    outgoing, arrived = slots[:chunks], slots[chunks:]
    me = lax.axis_index("shard")
    n_channels, n_samples = raw.shape
    padded = rounded.shape[0]
    half_rows = padded // 2
    home_rows = placed.shape[0]
    peers = records - 1
    firsts = [sum(GROUPS[:c]) for c in range(chunks + 1)]
    packed_rows = [ref.shape[1] for ref in outgoing]
    tap_rows = [sum(packed_rows[:c]) for c in range(chunks)]

    start = (lax.rem(me // 4, 2) * 2 + lax.rem(me, 2)) * peers // 4

    def turn(i):
        return peers - lax.rem(start + i, peers)

    def partner(step):
        if records & (records - 1):
            return lax.rem(me + step, records)
        other = 0
        bit = 1
        while bit < records:
            other = other + bit * lax.rem(me // bit + step // bit, 2)
            bit *= 2
        return other

    sem_count = [0]

    def load(source, target):
        copy = pltpu.make_async_copy(source, target, load_sem.at[sem_count[0]])
        sem_count[0] += 1
        copy.start()
        return copy

    def load_columns(c):
        lanes = pl.ds(firsts[c] * LANES, GROUPS[c] * LANES)
        return load(forward.at[:, lanes], table.at[:, lanes])

    piece = round_up(-(-n_channels // 3), 16)
    back_load = load(back_table, back)
    pieces = []
    for row in range(0, n_channels, piece):
        rows = pl.ds(row, min(piece, n_channels - row))
        pieces.append((row, load(traces.at[rows, :], raw.at[rows, :])))
    column_loads = [load_columns(0)]
    wave_load = load(wave_table, wave)
    vertical_load = load(vertical_table, vertical)

    barrier = pltpu.get_barrier_semaphore()
    for step in range(1, records):
        pl.semaphore_signal(
            barrier,
            inc=1,
            device_id={"shard": partner(step)},
            device_id_type=pl.DeviceIdType.MESH,
        )

    packed[...] = jnp.zeros_like(packed)
    rounded[n_channels // 16 * 16 :, :] = jnp.zeros_like(rounded[n_channels // 16 * 16 :, :])
    n_bins = home.shape[0]
    homes = home[...].reshape(1, n_bins)
    moved = homes
    for d in range(1, records):
        moved = moved + jnp.where(homes >= d * per_device, stride - per_device, 0)
    bins = lax.broadcasted_iota(jnp.int32, (n_bins, n_channels), 0)
    chosen = (bins == receiver[...].reshape(1, n_channels)).astype(jnp.bfloat16)
    back_load.wait()
    by_bin = jnp.dot(chosen, back[...], preferred_element_type=jnp.float32).astype(jnp.bfloat16)
    rows = lax.broadcasted_iota(jnp.int32, (home_rows, n_bins), 0)
    chosen = (rows == moved).astype(jnp.bfloat16)
    placed[...] = jnp.dot(chosen, by_bin, preferred_element_type=jnp.float32).astype(jnp.bfloat16)

    for row, copy in pieces:
        copy.wait()
        end = min(row + piece, n_channels)
        rounded[row:end, :] = raw[row:end, :].astype(jnp.bfloat16)
    column_loads += [load_columns(c) for c in range(1, chunks)]
    lag_load = load(taps, lag)
    inverse_load = load(inverse_table, inverse)

    total = jnp.zeros((8, LANES), jnp.float32)
    sends = []
    for c, group in enumerate(GROUPS):
        column_loads[c].wait()
        spectra[:, : group * LANES] = jnp.dot(
            rounded[...],
            table[:, firsts[c] * LANES : firsts[c + 1] * LANES],
            preferred_element_type=jnp.float32,
        ).astype(jnp.bfloat16)
        if c == 0:
            wave_load.wait()
        turned = jnp.dot(
            wave[...], spectra[:, : group * LANES], preferred_element_type=jnp.float32
        )
        if c == 0:
            vertical_load.wait()
        for b in range(group):
            lanes = slice(b * LANES, (b + 1) * LANES)
            column = firsts[c] + b
            straight, crossed = gain_tiles(
                vertical[:, column * LANES : (column + 1) * LANES], depth[0], n_channels
            )
            for part in range(2):
                part_rows = slice(part * half_rows, (part + 1) * half_rows)
                value = turned[part_rows, lanes]
                lifted[part_rows, lanes] = (
                    straight * value + crossed * pltpu.roll(value, HALF, 1)
                ).astype(jnp.bfloat16)
        cleaned = jnp.dot(
            placed[...], lifted[:, : group * LANES], preferred_element_type=jnp.float32
        )
        for b in range(group):
            block = cleaned[:, b * LANES : (b + 1) * LANES]
            total = total + jnp.sum((block * block).reshape(-1, 8, LANES), axis=0)
            for d in range(records):
                packed[d, b * per_device : (b + 1) * per_device, :] = block[
                    d * stride : d * stride + per_device
                ]
        outgoing[c][...] = packed[:, : packed_rows[c], :].astype(jnp.bfloat16)
        if c == 0:
            pl.semaphore_wait(barrier, peers)
        for i in range(peers):
            step = turn(i)
            other = partner(step)
            send = pltpu.make_async_remote_copy(
                src_ref=outgoing[c].at[other],
                dst_ref=arrived[c].at[me],
                send_sem=send_sem.at[c, step - 1],
                recv_sem=recv_sem.at[c, step - 1],
                device_id={"shard": other},
                device_id_type=pl.DeviceIdType.MESH,
            )
            send.start()
            sends.append(send)
        arrived[c][me] = outgoing[c][me]

    sums[me] = total
    for i in range(peers):
        step = turn(i)
        send = pltpu.make_async_remote_copy(
            src_ref=sums.at[me],
            dst_ref=sums.at[me],
            send_sem=sum_send.at[step - 1],
            recv_sem=sum_recv.at[step - 1],
            device_id={"shard": partner(step)},
            device_id_type=pl.DeviceIdType.MESH,
        )
        send.start()
        sends.append(send)

    order = []
    for q in range(records):
        place = jnp.int32(0)
        for s in range(records):
            place = jnp.where(shot_slot[s] == q, s, place)
        order.append(place)
    lag_load.wait()
    inverse_load.wait()
    tile = 16
    done = 0
    for c, group in enumerate(GROUPS):
        for send in sends[c * peers : (c + 1) * peers]:
            send.wait()

        def filter_rows(r, carry):
            at = pl.ds(pl.multiple_of(r * tile, tile), tile)
            tap_at = pl.ds(pl.multiple_of(tap_rows[c] + r * tile, tile), tile)
            values = [arrived[c][order[q], at, :].astype(jnp.float32) for q in range(records)]
            for p in range(records):
                result = None
                for q in range(records):
                    term = lag[abs(p - q), tap_at, :] * values[q]
                    result = term if result is None else result + term
                shots[p, at, :] = result
            return carry

        lax.fori_loop(0, packed_rows[c] // tile, filter_rows, 0)
        for b in range(group):
            for p in range(records):
                ordered[b, pl.ds(p, per_device, stride=records), :] = shots[
                    p, b * per_device : (b + 1) * per_device, :
                ]
            if c == chunks - 1:
                last[:, b * LANES : (b + 1) * LANES] = ordered[b].astype(jnp.bfloat16)
            else:
                column = firsts[c] + b
                filtered[:, column * LANES : (column + 1) * LANES] = ordered[b].astype(
                    jnp.bfloat16
                )
        if 0 < c < chunks - 1:
            depth_at = slice(done * LANES, firsts[c + 1] * LANES)
            for n in range(0, n_samples, 512):
                part = jnp.dot(
                    filtered[:, depth_at],
                    inverse[depth_at, n : n + 512],
                    preferred_element_type=jnp.float32,
                )
                if done:
                    part = summed[:, n : n + 512] + part
                summed[:, n : n + 512] = part
            done = firsts[c + 1]
        if c == chunks - 2:
            store = pltpu.make_async_copy(summed, partial, load_sem.at[sem_count[0]])
            store.start()
    for send in sends[chunks * peers :]:
        send.wait()
    energy[...] = jnp.sum(sums[...], axis=0)
    store.wait()


def exchange(traces, cable_depth, receiver, shot_slot, gather_home, tables, records):
    forward, inverse, wave, back, vertical, taps = tables
    back = back[: traces.shape[0]]
    n_channels, n_samples = traces.shape
    n_bins = gather_home.shape[0]
    per_device = n_bins // records
    stride = round_up(per_device, 16)
    padded = wave.shape[0]
    n_rows = per_device * records
    chunks = len(GROUPS)
    early = sum(GROUPS[:-1]) * LANES
    vmem = pl.BlockSpec(memory_space=pltpu.VMEM)
    smem = pl.BlockSpec(memory_space=pltpu.SMEM)
    anywhere = pl.BlockSpec(memory_space=pl.ANY)
    width = max(GROUPS) * LANES
    packed = [round_up(group * per_device, 16) for group in GROUPS]
    peers = records - 1
    slots = [pltpu.VMEM((records, rows, LANES), jnp.bfloat16) for rows in packed]
    return pl.pallas_call(
        functools.partial(exchange_kernel, records, per_device, stride),
        out_shape=(
            jax.ShapeDtypeStruct((n_rows, GROUPS[-1] * LANES), jnp.bfloat16),
            jax.ShapeDtypeStruct((8, LANES), jnp.float32),
            jax.ShapeDtypeStruct((n_rows, n_samples), jnp.float32),
        ),
        in_specs=[anywhere] * 7 + [smem, smem, vmem, vmem],
        out_specs=(vmem, vmem, anywhere),
        scratch_shapes=[
            pltpu.VMEM((n_channels, n_samples), jnp.float32),
            pltpu.VMEM((padded, n_samples), jnp.bfloat16),
            pltpu.VMEM(forward.shape, jnp.bfloat16),
            pltpu.VMEM(wave.shape, jnp.bfloat16),
            pltpu.VMEM(back.shape, jnp.bfloat16),
            pltpu.VMEM(vertical.shape, jnp.float32),
            pltpu.VMEM(taps.shape, jnp.float32),
            pltpu.VMEM((early, n_samples), jnp.bfloat16),
            pltpu.VMEM((records * stride, padded), jnp.bfloat16),
            pltpu.VMEM((padded, width), jnp.bfloat16),
            pltpu.VMEM((padded, width), jnp.bfloat16),
            pltpu.VMEM((records, max(packed), LANES), jnp.float32),
            pltpu.VMEM((records, max(packed), LANES), jnp.float32),
            pltpu.VMEM((max(GROUPS), n_rows, LANES), jnp.float32),
            pltpu.VMEM((n_rows, early), jnp.bfloat16),
            pltpu.VMEM((n_rows, n_samples), jnp.float32),
            pltpu.VMEM((records, 8, LANES), jnp.float32),
            pltpu.SemaphoreType.DMA((16,)),
            pltpu.SemaphoreType.DMA((chunks, peers)),
            pltpu.SemaphoreType.DMA((chunks, peers)),
            pltpu.SemaphoreType.DMA((peers,)),
            pltpu.SemaphoreType.DMA((peers,)),
        ]
        + slots
        + slots,
        compiler_params=pltpu.CompilerParams(
            collective_id=0, has_side_effects=True, vmem_limit_bytes=58 * 1024 * 1024
        ),
    )(
        traces,
        forward,
        wave,
        back,
        vertical,
        taps,
        inverse[:early],
        cable_depth,
        shot_slot,
        gather_home,
        receiver,
    )


def inverse_kernel(count, energy, partial, filtered, inverse, out):
    total = jnp.sum(energy[...])
    scale = lax.rsqrt(jnp.full((1, 1), 2.0 * FREQ, jnp.float32) * (total / count + energy_eps))
    out[...] = (
        partial[...] + jnp.dot(filtered[...], inverse[...], preferred_element_type=jnp.float32)
    ) * scale


def invert(partial, filtered, energy, inverse, count):
    n_rows, n_samples = partial.shape
    depth = filtered.shape[1]
    block = max(rows for rows in range(16, 129, 16) if n_rows % rows == 0)
    return pl.pallas_call(
        functools.partial(inverse_kernel, count),
        out_shape=jax.ShapeDtypeStruct((n_rows, n_samples), jnp.float32),
        grid=(n_rows // block,),
        in_specs=[
            pl.BlockSpec((8, LANES), lambda i: (0, 0)),
            pl.BlockSpec((block, n_samples), lambda i: (i, 0)),
            pl.BlockSpec((block, depth), lambda i: (i, 0)),
            pl.BlockSpec((depth, n_samples), lambda i: (0, 0)),
        ],
        out_specs=pl.BlockSpec((block, n_samples), lambda i: (i, 0)),
        compiler_params=pltpu.CompilerParams(vmem_limit_bytes=60 * 1024 * 1024),
    )(energy, partial, filtered, inverse[-depth:])


def fused_shards(traces, cable_depth, receiver, shot_slot, gather_home):
    records = lax.axis_size("shard")
    n_channels, n_samples = traces.shape
    per_device = gather_home.shape[0] // records
    tables = fused_tables(n_channels, n_samples, records, per_device)
    last, energy, partial = exchange(
        traces, cable_depth, receiver, shot_slot, gather_home, tables, records
    )
    out = invert(partial, last, energy, tables[1], float(n_channels * records * FREQ))
    return out.reshape(per_device, records, n_samples)


def solution(mesh):
    in_specs = (
        P(("groups", "shard"), None),
        P(("groups", "shard")),
        P(("groups", "shard")),
        P("groups"),
        P("groups"),
    )
    out_specs = P(("groups", "shard"), None, None)
    body = fused_shards if mesh.shape["shard"] <= 16 else shards
    return jax.shard_map(body, mesh=mesh, in_specs=in_specs, out_specs=out_specs, check_vma=False)
```

```python
import functools
import math

import jax
import jax.numpy as jnp
import ml_dtypes
import numpy as np
from jax import lax
from jax.experimental import pallas as pl
from jax.experimental.pallas import tpu as pltpu
from jax.sharding import PartitionSpec as P

FREQ = 576


sample_step = 0.002
water_speed = 1500.0
channel_spacing = 12.5
shot_spacing = 25.0
surface_reflect = 0.9
ghost_floor = 0.1
reject_speed = 1500.0
low_floor = 4.0 * math.pi
energy_eps = 1e-06


def forward_time(n_samples, first_bin, band_size):
    samples = jnp.arange(n_samples, dtype=jnp.int32)
    freq_bins = first_bin + jnp.arange(band_size, dtype=jnp.int32)
    angles = (samples[:, None] * freq_bins[None, :] % n_samples).astype(jnp.float32) * (
        2.0 * math.pi / n_samples
    )
    return jnp.concatenate([jnp.cos(angles), -jnp.sin(angles)], axis=1).astype(jnp.bfloat16)


def inverse_time(n_samples, first_bin, band_size):
    samples = jnp.arange(n_samples, dtype=jnp.int32)
    freq_bins = first_bin + jnp.arange(band_size, dtype=jnp.int32)
    angles = (freq_bins[:, None] * samples[None, :] % n_samples).astype(jnp.float32) * (
        2.0 * math.pi / n_samples
    )
    weights = jnp.where(freq_bins == 0, 1.0, 2.0).astype(jnp.float32)[:, None]
    return jnp.concatenate([weights * jnp.cos(angles), -weights * jnp.sin(angles)], axis=0).astype(
        jnp.bfloat16
    )


def wave_tables(n_channels):
    wave_index = jnp.arange(n_channels, dtype=jnp.int32)
    angles = (wave_index[:, None] * wave_index[None, :] % n_channels).astype(jnp.float32) * (
        2.0 * math.pi / n_channels
    )
    return (jnp.cos(angles).astype(jnp.bfloat16), jnp.sin(angles).astype(jnp.bfloat16))


def angular_band(n_samples, first_bin, band_size):
    freq_bins = (first_bin + jnp.arange(band_size, dtype=jnp.int32)).astype(jnp.float32)
    return 2.0 * math.pi * freq_bins / (n_samples * sample_step)


def ghost_operator(n_channels, n_samples, first_bin, band_size, depth_value):
    angular = angular_band(n_samples, first_bin, band_size)
    wave_index = jnp.arange(n_channels, dtype=jnp.int32)
    signed = jnp.where(wave_index <= n_channels // 2, wave_index, wave_index - n_channels).astype(
        jnp.float32
    )
    wave_number = 2.0 * math.pi * signed / (n_channels * channel_spacing)
    slowness = angular / water_speed
    vertical = jnp.sqrt(
        jnp.maximum(
            slowness[None, :] * slowness[None, :] - wave_number[:, None] * wave_number[:, None], 0.0
        )
    )
    angles = 2.0 * vertical * depth_value
    cosine = jnp.cos(angles)
    denominator = (
        1.0 - 2.0 * surface_reflect * cosine + surface_reflect * surface_reflect + ghost_floor
    )
    return (
        (1.0 - surface_reflect * cosine) / denominator,
        -surface_reflect * jnp.sin(angles) / denominator,
    )


def deghost(record, depth_value, first_bin, band_size):
    n_channels, n_samples = record.shape
    spectra = jnp.dot(
        record.astype(jnp.bfloat16),
        forward_time(n_samples, first_bin, band_size),
        preferred_element_type=jnp.float32,
    ).astype(jnp.bfloat16)
    cos_wave, sin_wave = wave_tables(n_channels)
    plain = jnp.dot(cos_wave, spectra, preferred_element_type=jnp.float32)
    turned = jnp.dot(sin_wave, spectra, preferred_element_type=jnp.float32)
    wave_re = plain[:, :band_size] + turned[:, band_size:]
    wave_im = plain[:, band_size:] - turned[:, :band_size]
    gain_re, gain_im = ghost_operator(n_channels, n_samples, first_bin, band_size, depth_value)
    lifted = jnp.concatenate(
        [gain_re * wave_re - gain_im * wave_im, gain_re * wave_im + gain_im * wave_re], axis=1
    ).astype(jnp.bfloat16)
    plain = jnp.dot(cos_wave, lifted, preferred_element_type=jnp.float32)
    turned = jnp.dot(sin_wave, lifted, preferred_element_type=jnp.float32)
    back_re = (plain[:, :band_size] - turned[:, band_size:]) / n_channels
    back_im = (plain[:, band_size:] + turned[:, :band_size]) / n_channels
    cleaned = jnp.concatenate([back_re, back_im], axis=1)
    return (cleaned.astype(jnp.bfloat16), jnp.sum(cleaned * cleaned))


def shot_tables(positions, records):
    wave_index = jnp.arange(2 * records, dtype=jnp.int32)
    angles = (positions[:, None] * wave_index[None, :] % (2 * records)).astype(jnp.float32) * (
        math.pi / records
    )
    return (jnp.cos(angles).astype(jnp.bfloat16), jnp.sin(angles).astype(jnp.bfloat16))


def shot_filter(records, n_samples, first_bin, band_size):
    angular = angular_band(n_samples, first_bin, band_size)
    wave_index = jnp.arange(2 * records, dtype=jnp.int32)
    signed = jnp.where(wave_index <= records, wave_index, wave_index - 2 * records).astype(
        jnp.float32
    )
    shot_number = 2.0 * math.pi * signed / (2 * records * shot_spacing)
    reject_ratio = reject_speed * jnp.abs(shot_number)[:, None] / (angular[None, :] + low_floor)
    squared = reject_ratio * reject_ratio
    response = 1.0 / (1.0 + squared * squared) / (2.0 * records)
    return jnp.concatenate([response, response], axis=1)


def place_rows(clean_rows, receiver, gather_home, records, per_device):
    targets = jnp.take(gather_home, receiver, axis=0)
    buffer = (
        jnp.zeros((records * per_device, clean_rows.shape[1]), jnp.bfloat16)
        .at[targets]
        .set(clean_rows)
    )
    return buffer.reshape(records, per_device, clean_rows.shape[1])


def filter_gathers(arrived, shot_slot, n_samples, first_bin, band_size):
    records = arrived.shape[0]
    cos_source, sin_source = shot_tables(shot_slot, records)
    cos_shot, sin_shot = shot_tables(jnp.arange(records, dtype=jnp.int32), records)
    response = shot_filter(records, n_samples, first_bin, band_size)[:, None, :]
    even_part = (
        jnp.einsum("sgf,sk->kgf", arrived, cos_source, preferred_element_type=jnp.float32)
        * response
    ).astype(jnp.bfloat16)
    odd_part = (
        jnp.einsum("sgf,sk->kgf", arrived, sin_source, preferred_element_type=jnp.float32)
        * response
    ).astype(jnp.bfloat16)
    filtered = (
        jnp.einsum("pk,kgf->gpf", cos_shot, even_part, preferred_element_type=jnp.float32)
        + jnp.einsum("pk,kgf->gpf", sin_shot, odd_part, preferred_element_type=jnp.float32)
    ).astype(jnp.bfloat16)
    return jnp.einsum(
        "gpf,ft->gpt",
        filtered,
        inverse_time(n_samples, first_bin, band_size),
        preferred_element_type=jnp.float32,
    )


def shards(traces, cable_depth, receiver, shot_slot, gather_home):
    records = lax.axis_size("shard")
    per_device = gather_home.shape[0] // records
    n_channels, n_samples = traces.shape
    clean_rows, energy = deghost(traces, cable_depth[0], 0, FREQ)
    outgoing = place_rows(clean_rows, receiver, gather_home, records, per_device)
    arrived = lax.all_to_all(outgoing, "shard", split_axis=0, concat_axis=0, tiled=True)
    summed = filter_gathers(arrived, shot_slot, n_samples, 0, FREQ)
    total_energy = lax.psum(energy, "shard")
    out_scale = 1.0 / jnp.sqrt(
        2.0 * FREQ * (total_energy / (n_channels * records * FREQ) + energy_eps)
    )
    return summed * out_scale


def round_up(value, unit):
    return -(-value // unit) * unit


LANES = 128
HALF = LANES // 2
GROUPS = (1, 3, 3, 2)


def fused_tables(n_channels, n_samples, records, per_device):
    bf16 = ml_dtypes.bfloat16
    blocks = FREQ // HALF
    bins = np.arange(FREQ).reshape(blocks, HALF)
    samples = np.arange(n_samples)
    turn = 2.0 * np.pi / n_samples
    angle = (samples[:, None] * np.arange(FREQ)[None, :] % n_samples) * turn
    cos_t = np.cos(angle).reshape(n_samples, blocks, 1, HALF)
    sin_t = np.sin(angle).reshape(n_samples, blocks, 1, HALF)
    forward = np.concatenate([cos_t, -sin_t], axis=2).reshape(n_samples, blocks * LANES)
    weight = np.where(bins == 0, 1.0, 2.0)[None, :, None, :]
    inverse = np.concatenate([weight * cos_t, -weight * sin_t], axis=2)
    inverse = inverse.reshape(n_samples, blocks * LANES).T
    half_rows = round_up(n_channels // 2 + 1, 16)
    wave = np.zeros((2 * half_rows, 2 * half_rows))
    index = np.arange(n_channels // 2 + 1)
    angle = (index[:, None] * np.arange(n_channels)[None, :] % n_channels) * (
        2.0 * np.pi / n_channels
    )
    wave[: index.size, :n_channels] = np.cos(angle)
    wave[half_rows : half_rows + index.size, :n_channels] = np.sin(angle)
    own_mirror = (index * 2) % n_channels == 0
    wave[half_rows : half_rows + index.size][own_mirror] = 0.0
    twice = np.ones((2 * half_rows, 1))
    twice[: index.size, 0] = np.where(own_mirror, 1.0, 2.0)
    twice[half_rows : half_rows + index.size, 0] = 2.0
    wave = wave.astype(bf16)
    back = (wave.astype(np.float64) * twice).T.astype(bf16)

    angular = 2.0 * np.pi * np.arange(FREQ) / (n_samples * sample_step)
    number = 2.0 * np.pi * np.arange(half_rows) / (n_channels * channel_spacing)
    vertical = np.sqrt(
        np.maximum((angular / water_speed)[None, :] ** 2 - number[:, None] ** 2, 0.0)
    )
    vertical = (vertical / np.pi).reshape(half_rows, blocks, 1, HALF)
    vertical = np.concatenate([vertical, vertical], axis=2).reshape(half_rows, blocks * LANES)

    shots = np.arange(2 * records)
    signed = np.where(shots <= records, shots, shots - 2 * records)
    shot_number = 2.0 * np.pi * signed / (2 * records * shot_spacing)
    ratio = reject_speed * np.abs(shot_number)[:, None] / (angular[None, :] + low_floor)
    response = 1.0 / (1.0 + ratio**4) / (2.0 * records)
    apart = np.arange(records)
    lag = np.cos(np.pi / records * (apart[:, None] * shots[None, :] % (2 * records))) @ response
    lag = lag.reshape(records, blocks, 1, HALF)
    lag = np.concatenate([lag, lag], axis=2).reshape(records, blocks, 1, LANES)
    lag = np.broadcast_to(lag, (records, blocks, per_device, LANES))
    taps = []
    first = 0
    for group in GROUPS:
        filled = group * per_device
        part = np.zeros((records, round_up(filled, 16), LANES))
        part[:, :filled] = lag[:, first : first + group].reshape(records, filled, LANES)
        taps.append(part)
        first += group
    taps = np.concatenate(taps, axis=1)
    return (
        forward.astype(bf16),
        inverse.astype(bf16),
        wave,
        back,
        vertical.astype(np.float32),
        taps.astype(np.float32),
    )


SINE = [(-1.0) ** i * (2.0 * math.pi) ** (2 * i + 1) / math.factorial(2 * i + 1) for i in range(6)]


def gain_tiles(vertical, depth, n_channels):
    left = lax.broadcasted_iota(jnp.int32, vertical.shape, 1) < HALF
    turns = vertical * depth - jnp.where(left, 0.25, 0.0)
    offset = 0.25 - jnp.abs(turns - jnp.floor(turns + 0.5))
    square = offset * offset
    value = jnp.full_like(square, SINE[-1])
    for coefficient in SINE[-2::-1]:
        value = value * square + coefficient
    value = value * offset
    swapped = pltpu.roll(value, HALF, 1)
    cosine = jnp.where(left, swapped, value)
    sine = jnp.where(left, value, -swapped)
    denominator = (
        1.0 - 2.0 * surface_reflect * cosine + surface_reflect * surface_reflect + ghost_floor
    )
    scale = 1.0 / (denominator * n_channels)
    return (1.0 - surface_reflect * cosine) * scale, surface_reflect * sine * scale


def exchange_kernel(
    records,
    per_device,
    stride,
    traces,
    forward,
    wave_table,
    back_table,
    vertical_table,
    taps,
    inverse_table,
    depth,
    shot_slot,
    home,
    receiver,
    last,
    energy,
    summed,
    raw,
    rounded,
    table,
    wave,
    back,
    vertical,
    lag,
    inverse,
    placed,
    spectra,
    lifted,
    packed,
    shots,
    ordered,
    filtered,
    sums,
    load_sem,
    send_sem,
    recv_sem,
    sum_send,
    sum_recv,
    *slots,
):
    chunks = len(GROUPS)
    outgoing, arrived = slots[:chunks], slots[chunks:]
    me = lax.axis_index("shard")
    n_channels, n_samples = raw.shape
    padded = rounded.shape[0]
    half_rows = padded // 2
    home_rows = placed.shape[0]
    peers = records - 1
    firsts = [sum(GROUPS[:c]) for c in range(chunks + 1)]
    packed_rows = [ref.shape[1] for ref in outgoing]
    tap_rows = [sum(packed_rows[:c]) for c in range(chunks)]

    start = (lax.rem(me // 4, 2) * 2 + lax.rem(me, 2)) * peers // 4

    def turn(i):
        return peers - lax.rem(start + i, peers)

    def partner(step):
        if records & (records - 1):
            return lax.rem(me + step, records)
        other = 0
        bit = 1
        while bit < records:
            other = other + bit * lax.rem(me // bit + step // bit, 2)
            bit *= 2
        return other

    sem_count = [0]

    def load(source, target):
        copy = pltpu.make_async_copy(source, target, load_sem.at[sem_count[0]])
        sem_count[0] += 1
        copy.start()
        return copy

    def load_columns(c):
        lanes = pl.ds(firsts[c] * LANES, GROUPS[c] * LANES)
        return load(forward.at[:, lanes], table.at[:, lanes])

    piece = round_up(-(-n_channels // 3), 16)
    back_load = load(back_table, back)
    pieces = []
    for row in range(0, n_channels, piece):
        rows = pl.ds(row, min(piece, n_channels - row))
        pieces.append((row, load(traces.at[rows, :], raw.at[rows, :])))
    column_loads = [load_columns(0)]
    wave_load = load(wave_table, wave)
    vertical_load = load(vertical_table, vertical)

    barrier = pltpu.get_barrier_semaphore()
    for step in range(1, records):
        pl.semaphore_signal(
            barrier,
            inc=1,
            device_id={"shard": partner(step)},
            device_id_type=pl.DeviceIdType.MESH,
        )

    packed[...] = jnp.zeros_like(packed)
    rounded[n_channels // 16 * 16 :, :] = jnp.zeros_like(rounded[n_channels // 16 * 16 :, :])
    n_bins = home.shape[0]
    homes = home[...].reshape(1, n_bins)
    moved = homes
    for d in range(1, records):
        moved = moved + jnp.where(homes >= d * per_device, stride - per_device, 0)
    bins = lax.broadcasted_iota(jnp.int32, (n_bins, n_channels), 0)
    chosen = (bins == receiver[...].reshape(1, n_channels)).astype(jnp.bfloat16)
    back_load.wait()
    by_bin = jnp.dot(chosen, back[...], preferred_element_type=jnp.float32).astype(jnp.bfloat16)
    rows = lax.broadcasted_iota(jnp.int32, (home_rows, n_bins), 0)
    chosen = (rows == moved).astype(jnp.bfloat16)
    placed[...] = jnp.dot(chosen, by_bin, preferred_element_type=jnp.float32).astype(jnp.bfloat16)

    for row, copy in pieces:
        copy.wait()
        end = min(row + piece, n_channels)
        rounded[row:end, :] = raw[row:end, :].astype(jnp.bfloat16)
    column_loads += [load_columns(c) for c in range(1, chunks)]
    lag_load = load(taps, lag)
    inverse_load = load(inverse_table, inverse)

    total = jnp.zeros((8, LANES), jnp.float32)
    sends = []
    for c, group in enumerate(GROUPS):
        column_loads[c].wait()
        spectra[:, : group * LANES] = jnp.dot(
            rounded[...],
            table[:, firsts[c] * LANES : firsts[c + 1] * LANES],
            preferred_element_type=jnp.float32,
        ).astype(jnp.bfloat16)
        if c == 0:
            wave_load.wait()
        turned = jnp.dot(
            wave[...], spectra[:, : group * LANES], preferred_element_type=jnp.float32
        )
        if c == 0:
            vertical_load.wait()
        for b in range(group):
            lanes = slice(b * LANES, (b + 1) * LANES)
            column = firsts[c] + b
            straight, crossed = gain_tiles(
                vertical[:, column * LANES : (column + 1) * LANES], depth[0], n_channels
            )
            for part in range(2):
                part_rows = slice(part * half_rows, (part + 1) * half_rows)
                value = turned[part_rows, lanes]
                lifted[part_rows, lanes] = (
                    straight * value + crossed * pltpu.roll(value, HALF, 1)
                ).astype(jnp.bfloat16)
        cleaned = jnp.dot(
            placed[...], lifted[:, : group * LANES], preferred_element_type=jnp.float32
        )
        for b in range(group):
            block = cleaned[:, b * LANES : (b + 1) * LANES]
            total = total + jnp.sum((block * block).reshape(-1, 8, LANES), axis=0)
            for d in range(records):
                packed[d, b * per_device : (b + 1) * per_device, :] = block[
                    d * stride : d * stride + per_device
                ]
        outgoing[c][...] = packed[:, : packed_rows[c], :].astype(jnp.bfloat16)
        if c == 0:
            pl.semaphore_wait(barrier, peers)
        for i in range(peers):
            step = turn(i)
            other = partner(step)
            send = pltpu.make_async_remote_copy(
                src_ref=outgoing[c].at[other],
                dst_ref=arrived[c].at[me],
                send_sem=send_sem.at[c, step - 1],
                recv_sem=recv_sem.at[c, step - 1],
                device_id={"shard": other},
                device_id_type=pl.DeviceIdType.MESH,
            )
            send.start()
            sends.append(send)
        arrived[c][me] = outgoing[c][me]

    sums[me] = total
    for i in range(peers):
        step = turn(i)
        send = pltpu.make_async_remote_copy(
            src_ref=sums.at[me],
            dst_ref=sums.at[me],
            send_sem=sum_send.at[step - 1],
            recv_sem=sum_recv.at[step - 1],
            device_id={"shard": partner(step)},
            device_id_type=pl.DeviceIdType.MESH,
        )
        send.start()
        sends.append(send)

    order = []
    for q in range(records):
        place = jnp.int32(0)
        for s in range(records):
            place = jnp.where(shot_slot[s] == q, s, place)
        order.append(place)
    lag_load.wait()
    inverse_load.wait()
    tile = 16
    done = 0
    for c, group in enumerate(GROUPS):
        for send in sends[c * peers : (c + 1) * peers]:
            send.wait()

        def filter_rows(r, carry):
            at = pl.ds(pl.multiple_of(r * tile, tile), tile)
            tap_at = pl.ds(pl.multiple_of(tap_rows[c] + r * tile, tile), tile)
            values = [arrived[c][order[q], at, :].astype(jnp.float32) for q in range(records)]
            for p in range(records):
                result = None
                for q in range(records):
                    term = lag[abs(p - q), tap_at, :] * values[q]
                    result = term if result is None else result + term
                shots[p, at, :] = result
            return carry

        lax.fori_loop(0, packed_rows[c] // tile, filter_rows, 0)
        for b in range(group):
            for p in range(records):
                ordered[b, pl.ds(p, per_device, stride=records), :] = shots[
                    p, b * per_device : (b + 1) * per_device, :
                ]
            if c == chunks - 1:
                last[:, b * LANES : (b + 1) * LANES] = ordered[b].astype(jnp.bfloat16)
            else:
                column = firsts[c] + b
                filtered[:, column * LANES : (column + 1) * LANES] = ordered[b].astype(
                    jnp.bfloat16
                )
        if 0 < c < chunks - 1:
            depth_at = slice(done * LANES, firsts[c + 1] * LANES)
            for n in range(0, n_samples, 512):
                part = jnp.dot(
                    filtered[:, depth_at],
                    inverse[depth_at, n : n + 512],
                    preferred_element_type=jnp.float32,
                )
                if done:
                    part = summed[:, n : n + 512] + part
                summed[:, n : n + 512] = part
            done = firsts[c + 1]
    for send in sends[chunks * peers :]:
        send.wait()
    energy[...] = jnp.sum(sums[...], axis=0)


def exchange(traces, cable_depth, receiver, shot_slot, gather_home, tables, records):
    forward, inverse, wave, back, vertical, taps = tables
    back = back[: traces.shape[0]]
    n_channels, n_samples = traces.shape
    n_bins = gather_home.shape[0]
    per_device = n_bins // records
    stride = round_up(per_device, 16)
    padded = wave.shape[0]
    n_rows = per_device * records
    chunks = len(GROUPS)
    early = sum(GROUPS[:-1]) * LANES
    vmem = pl.BlockSpec(memory_space=pltpu.VMEM)
    smem = pl.BlockSpec(memory_space=pltpu.SMEM)
    anywhere = pl.BlockSpec(memory_space=pl.ANY)
    width = max(GROUPS) * LANES
    packed = [round_up(group * per_device, 16) for group in GROUPS]
    peers = records - 1
    slots = [pltpu.VMEM((records, rows, LANES), jnp.bfloat16) for rows in packed]
    return pl.pallas_call(
        functools.partial(exchange_kernel, records, per_device, stride),
        out_shape=(
            pltpu.VMEM((n_rows, GROUPS[-1] * LANES), jnp.bfloat16),
            pltpu.VMEM((8, LANES), jnp.float32),
            pltpu.VMEM((n_rows, n_samples), jnp.float32),
        ),
        in_specs=[anywhere] * 7 + [smem, smem, vmem, vmem],
        out_specs=(vmem, vmem, vmem),
        scratch_shapes=[
            pltpu.VMEM((n_channels, n_samples), jnp.float32),
            pltpu.VMEM((padded, n_samples), jnp.bfloat16),
            pltpu.VMEM(forward.shape, jnp.bfloat16),
            pltpu.VMEM(wave.shape, jnp.bfloat16),
            pltpu.VMEM(back.shape, jnp.bfloat16),
            pltpu.VMEM(vertical.shape, jnp.float32),
            pltpu.VMEM(taps.shape, jnp.float32),
            pltpu.VMEM((early, n_samples), jnp.bfloat16),
            pltpu.VMEM((records * stride, padded), jnp.bfloat16),
            pltpu.VMEM((padded, width), jnp.bfloat16),
            pltpu.VMEM((padded, width), jnp.bfloat16),
            pltpu.VMEM((records, max(packed), LANES), jnp.float32),
            pltpu.VMEM((records, max(packed), LANES), jnp.float32),
            pltpu.VMEM((max(GROUPS), n_rows, LANES), jnp.float32),
            pltpu.VMEM((n_rows, early), jnp.bfloat16),
            pltpu.VMEM((records, 8, LANES), jnp.float32),
            pltpu.SemaphoreType.DMA((16,)),
            pltpu.SemaphoreType.DMA((chunks, peers)),
            pltpu.SemaphoreType.DMA((chunks, peers)),
            pltpu.SemaphoreType.DMA((peers,)),
            pltpu.SemaphoreType.DMA((peers,)),
        ]
        + slots
        + slots,
        compiler_params=pltpu.CompilerParams(
            collective_id=0, has_side_effects=True, vmem_limit_bytes=54 * 1024 * 1024
        ),
    )(
        traces,
        forward,
        wave,
        back,
        vertical,
        taps,
        inverse[:early],
        cable_depth,
        shot_slot,
        gather_home,
        receiver,
    )


def inverse_kernel(count, block, energy, partial, filtered, inverse, out, staged, sems):
    total = jnp.sum(energy[...])
    scale = lax.rsqrt(jnp.full((1, 1), 2.0 * FREQ, jnp.float32) * (total / count + energy_eps))
    stores = []
    for i, row in enumerate(range(0, partial.shape[0], block)):
        rows = slice(row, row + block)
        staged[rows, :] = (
            partial[rows, :]
            + jnp.dot(filtered[rows, :], inverse[...], preferred_element_type=jnp.float32)
        ) * scale
        store = pltpu.make_async_copy(
            staged.at[pl.ds(row, block), :], out.at[pl.ds(row, block), :], sems.at[i]
        )
        store.start()
        stores.append(store)
    for store in stores:
        store.wait()


def invert(partial, filtered, energy, inverse, count):
    n_rows, n_samples = partial.shape
    depth = filtered.shape[1]
    block = max(rows for rows in range(16, 129, 16) if n_rows % rows == 0)
    vmem = pl.BlockSpec(memory_space=pltpu.VMEM)
    return pl.pallas_call(
        functools.partial(inverse_kernel, count, block),
        out_shape=jax.ShapeDtypeStruct((n_rows, n_samples), jnp.float32),
        in_specs=[vmem] * 4,
        out_specs=pl.BlockSpec(memory_space=pl.ANY),
        scratch_shapes=[
            pltpu.VMEM((n_rows, n_samples), jnp.float32),
            pltpu.SemaphoreType.DMA((n_rows // block,)),
        ],
        compiler_params=pltpu.CompilerParams(vmem_limit_bytes=40 * 1024 * 1024),
    )(energy, partial, filtered, inverse[-depth:])


def fused_shards(traces, cable_depth, receiver, shot_slot, gather_home):
    records = lax.axis_size("shard")
    n_channels, n_samples = traces.shape
    per_device = gather_home.shape[0] // records
    tables = fused_tables(n_channels, n_samples, records, per_device)
    last, energy, partial = exchange(
        traces, cable_depth, receiver, shot_slot, gather_home, tables, records
    )
    out = invert(partial, last, energy, tables[1], float(n_channels * records * FREQ))
    return out.reshape(per_device, records, n_samples)


def solution(mesh):
    in_specs = (
        P(("groups", "shard"), None),
        P(("groups", "shard")),
        P(("groups", "shard")),
        P("groups"),
        P("groups"),
    )
    out_specs = P(("groups", "shard"), None, None)
    body = fused_shards if mesh.shape["shard"] <= 16 else shards
    return jax.shard_map(body, mesh=mesh, in_specs=in_specs, out_specs=out_specs, check_vma=False)
```

```python
import functools
import math

import jax
import jax.numpy as jnp
import ml_dtypes
import numpy as np
from jax import lax
from jax.experimental import pallas as pl
from jax.experimental.pallas import tpu as pltpu
from jax.sharding import PartitionSpec as P

FREQ = 576


sample_step = 0.002
water_speed = 1500.0
channel_spacing = 12.5
shot_spacing = 25.0
surface_reflect = 0.9
ghost_floor = 0.1
reject_speed = 1500.0
low_floor = 4.0 * math.pi
energy_eps = 1e-06


def forward_time(n_samples, first_bin, band_size):
    samples = jnp.arange(n_samples, dtype=jnp.int32)
    freq_bins = first_bin + jnp.arange(band_size, dtype=jnp.int32)
    angles = (samples[:, None] * freq_bins[None, :] % n_samples).astype(jnp.float32) * (
        2.0 * math.pi / n_samples
    )
    return jnp.concatenate([jnp.cos(angles), -jnp.sin(angles)], axis=1).astype(jnp.bfloat16)


def inverse_time(n_samples, first_bin, band_size):
    samples = jnp.arange(n_samples, dtype=jnp.int32)
    freq_bins = first_bin + jnp.arange(band_size, dtype=jnp.int32)
    angles = (freq_bins[:, None] * samples[None, :] % n_samples).astype(jnp.float32) * (
        2.0 * math.pi / n_samples
    )
    weights = jnp.where(freq_bins == 0, 1.0, 2.0).astype(jnp.float32)[:, None]
    return jnp.concatenate([weights * jnp.cos(angles), -weights * jnp.sin(angles)], axis=0).astype(
        jnp.bfloat16
    )


def wave_tables(n_channels):
    wave_index = jnp.arange(n_channels, dtype=jnp.int32)
    angles = (wave_index[:, None] * wave_index[None, :] % n_channels).astype(jnp.float32) * (
        2.0 * math.pi / n_channels
    )
    return (jnp.cos(angles).astype(jnp.bfloat16), jnp.sin(angles).astype(jnp.bfloat16))


def angular_band(n_samples, first_bin, band_size):
    freq_bins = (first_bin + jnp.arange(band_size, dtype=jnp.int32)).astype(jnp.float32)
    return 2.0 * math.pi * freq_bins / (n_samples * sample_step)


def ghost_operator(n_channels, n_samples, first_bin, band_size, depth_value):
    angular = angular_band(n_samples, first_bin, band_size)
    wave_index = jnp.arange(n_channels, dtype=jnp.int32)
    signed = jnp.where(wave_index <= n_channels // 2, wave_index, wave_index - n_channels).astype(
        jnp.float32
    )
    wave_number = 2.0 * math.pi * signed / (n_channels * channel_spacing)
    slowness = angular / water_speed
    vertical = jnp.sqrt(
        jnp.maximum(
            slowness[None, :] * slowness[None, :] - wave_number[:, None] * wave_number[:, None], 0.0
        )
    )
    angles = 2.0 * vertical * depth_value
    cosine = jnp.cos(angles)
    denominator = (
        1.0 - 2.0 * surface_reflect * cosine + surface_reflect * surface_reflect + ghost_floor
    )
    return (
        (1.0 - surface_reflect * cosine) / denominator,
        -surface_reflect * jnp.sin(angles) / denominator,
    )


def deghost(record, depth_value, first_bin, band_size):
    n_channels, n_samples = record.shape
    spectra = jnp.dot(
        record.astype(jnp.bfloat16),
        forward_time(n_samples, first_bin, band_size),
        preferred_element_type=jnp.float32,
    ).astype(jnp.bfloat16)
    cos_wave, sin_wave = wave_tables(n_channels)
    plain = jnp.dot(cos_wave, spectra, preferred_element_type=jnp.float32)
    turned = jnp.dot(sin_wave, spectra, preferred_element_type=jnp.float32)
    wave_re = plain[:, :band_size] + turned[:, band_size:]
    wave_im = plain[:, band_size:] - turned[:, :band_size]
    gain_re, gain_im = ghost_operator(n_channels, n_samples, first_bin, band_size, depth_value)
    lifted = jnp.concatenate(
        [gain_re * wave_re - gain_im * wave_im, gain_re * wave_im + gain_im * wave_re], axis=1
    ).astype(jnp.bfloat16)
    plain = jnp.dot(cos_wave, lifted, preferred_element_type=jnp.float32)
    turned = jnp.dot(sin_wave, lifted, preferred_element_type=jnp.float32)
    back_re = (plain[:, :band_size] - turned[:, band_size:]) / n_channels
    back_im = (plain[:, band_size:] + turned[:, :band_size]) / n_channels
    cleaned = jnp.concatenate([back_re, back_im], axis=1)
    return (cleaned.astype(jnp.bfloat16), jnp.sum(cleaned * cleaned))


def shot_tables(positions, records):
    wave_index = jnp.arange(2 * records, dtype=jnp.int32)
    angles = (positions[:, None] * wave_index[None, :] % (2 * records)).astype(jnp.float32) * (
        math.pi / records
    )
    return (jnp.cos(angles).astype(jnp.bfloat16), jnp.sin(angles).astype(jnp.bfloat16))


def shot_filter(records, n_samples, first_bin, band_size):
    angular = angular_band(n_samples, first_bin, band_size)
    wave_index = jnp.arange(2 * records, dtype=jnp.int32)
    signed = jnp.where(wave_index <= records, wave_index, wave_index - 2 * records).astype(
        jnp.float32
    )
    shot_number = 2.0 * math.pi * signed / (2 * records * shot_spacing)
    reject_ratio = reject_speed * jnp.abs(shot_number)[:, None] / (angular[None, :] + low_floor)
    squared = reject_ratio * reject_ratio
    response = 1.0 / (1.0 + squared * squared) / (2.0 * records)
    return jnp.concatenate([response, response], axis=1)


def place_rows(clean_rows, receiver, gather_home, records, per_device):
    targets = jnp.take(gather_home, receiver, axis=0)
    buffer = (
        jnp.zeros((records * per_device, clean_rows.shape[1]), jnp.bfloat16)
        .at[targets]
        .set(clean_rows)
    )
    return buffer.reshape(records, per_device, clean_rows.shape[1])


def filter_gathers(arrived, shot_slot, n_samples, first_bin, band_size):
    records = arrived.shape[0]
    cos_source, sin_source = shot_tables(shot_slot, records)
    cos_shot, sin_shot = shot_tables(jnp.arange(records, dtype=jnp.int32), records)
    response = shot_filter(records, n_samples, first_bin, band_size)[:, None, :]
    even_part = (
        jnp.einsum("sgf,sk->kgf", arrived, cos_source, preferred_element_type=jnp.float32)
        * response
    ).astype(jnp.bfloat16)
    odd_part = (
        jnp.einsum("sgf,sk->kgf", arrived, sin_source, preferred_element_type=jnp.float32)
        * response
    ).astype(jnp.bfloat16)
    filtered = (
        jnp.einsum("pk,kgf->gpf", cos_shot, even_part, preferred_element_type=jnp.float32)
        + jnp.einsum("pk,kgf->gpf", sin_shot, odd_part, preferred_element_type=jnp.float32)
    ).astype(jnp.bfloat16)
    return jnp.einsum(
        "gpf,ft->gpt",
        filtered,
        inverse_time(n_samples, first_bin, band_size),
        preferred_element_type=jnp.float32,
    )


def shards(traces, cable_depth, receiver, shot_slot, gather_home):
    records = lax.axis_size("shard")
    per_device = gather_home.shape[0] // records
    n_channels, n_samples = traces.shape
    clean_rows, energy = deghost(traces, cable_depth[0], 0, FREQ)
    outgoing = place_rows(clean_rows, receiver, gather_home, records, per_device)
    arrived = lax.all_to_all(outgoing, "shard", split_axis=0, concat_axis=0, tiled=True)
    summed = filter_gathers(arrived, shot_slot, n_samples, 0, FREQ)
    total_energy = lax.psum(energy, "shard")
    out_scale = 1.0 / jnp.sqrt(
        2.0 * FREQ * (total_energy / (n_channels * records * FREQ) + energy_eps)
    )
    return summed * out_scale


def round_up(value, unit):
    return -(-value // unit) * unit


LANES = 128
HALF = LANES // 2
GROUPS = (2, 2, 2, 2, 1)


def band_rows(per_device):
    ends = [sum(GROUPS[: c + 1]) * per_device for c in range(len(GROUPS))]
    return [0] + [end // 16 * 16 for end in ends[:-1]] + [round_up(ends[-1], 16)]


def fused_tables(n_channels, n_samples, records, per_device):
    bf16 = ml_dtypes.bfloat16
    blocks = FREQ // HALF
    bins = np.arange(FREQ).reshape(blocks, HALF)
    samples = np.arange(n_samples)
    turn = 2.0 * np.pi / n_samples
    angle = (samples[:, None] * np.arange(FREQ)[None, :] % n_samples) * turn
    cos_t = np.cos(angle).reshape(n_samples, blocks, 1, HALF)
    sin_t = np.sin(angle).reshape(n_samples, blocks, 1, HALF)
    forward = np.concatenate([cos_t, -sin_t], axis=2).reshape(n_samples, blocks * LANES)
    weight = np.where(bins == 0, 1.0, 2.0)[None, :, None, :]
    inverse = np.concatenate([weight * cos_t, -weight * sin_t], axis=2)
    inverse = inverse.reshape(n_samples, blocks * LANES).T
    half_rows = round_up(n_channels // 2 + 1, 16)
    wave = np.zeros((2 * half_rows, 2 * half_rows))
    index = np.arange(n_channels // 2 + 1)
    angle = (index[:, None] * np.arange(n_channels)[None, :] % n_channels) * (
        2.0 * np.pi / n_channels
    )
    wave[: index.size, :n_channels] = np.cos(angle)
    wave[half_rows : half_rows + index.size, :n_channels] = np.sin(angle)
    own_mirror = (index * 2) % n_channels == 0
    wave[half_rows : half_rows + index.size][own_mirror] = 0.0
    twice = np.ones((2 * half_rows, 1))
    twice[: index.size, 0] = np.where(own_mirror, 1.0, 2.0)
    twice[half_rows : half_rows + index.size, 0] = 2.0
    wave = wave.astype(bf16)
    back = (wave.astype(np.float64) * twice).T.astype(bf16)

    angular = 2.0 * np.pi * np.arange(FREQ) / (n_samples * sample_step)
    number = 2.0 * np.pi * np.arange(half_rows) / (n_channels * channel_spacing)
    vertical = np.sqrt(
        np.maximum((angular / water_speed)[None, :] ** 2 - number[:, None] ** 2, 0.0)
    )
    vertical = (vertical / np.pi).reshape(half_rows, blocks, 1, HALF)
    vertical = np.concatenate([vertical, vertical], axis=2).reshape(half_rows, blocks * LANES)

    shots = np.arange(2 * records)
    signed = np.where(shots <= records, shots, shots - 2 * records)
    shot_number = 2.0 * np.pi * signed / (2 * records * shot_spacing)
    ratio = reject_speed * np.abs(shot_number)[:, None] / (angular[None, :] + low_floor)
    response = 1.0 / (1.0 + ratio**4) / (2.0 * records)
    apart = np.arange(records)
    lag = np.cos(np.pi / records * (apart[:, None] * shots[None, :] % (2 * records))) @ response
    lag = lag.reshape(records, blocks, 1, HALF)
    lag = np.concatenate([lag, lag], axis=2).reshape(records, blocks, 1, LANES)
    lag = np.broadcast_to(lag, (records, blocks, per_device, LANES))
    taps = np.zeros((records, band_rows(per_device)[-1], LANES))
    taps[:, : blocks * per_device] = lag.reshape(records, blocks * per_device, LANES)
    return (
        forward.astype(bf16),
        inverse.astype(bf16),
        wave,
        back,
        vertical.astype(np.float32),
        taps.astype(np.float32),
    )


SINE = [(-1.0) ** i * (2.0 * math.pi) ** (2 * i + 1) / math.factorial(2 * i + 1) for i in range(6)]


def gain_tiles(vertical, depth, n_channels):
    left = lax.broadcasted_iota(jnp.int32, vertical.shape, 1) < HALF
    turns = vertical * depth - jnp.where(left, 0.25, 0.0)
    offset = 0.25 - jnp.abs(turns - jnp.floor(turns + 0.5))
    square = offset * offset
    value = jnp.full_like(square, SINE[-1])
    for coefficient in SINE[-2::-1]:
        value = value * square + coefficient
    value = value * offset
    swapped = pltpu.roll(value, HALF, 1)
    cosine = jnp.where(left, swapped, value)
    sine = jnp.where(left, value, -swapped)
    denominator = (
        1.0 - 2.0 * surface_reflect * cosine + surface_reflect * surface_reflect + ghost_floor
    )
    scale = 1.0 / (denominator * n_channels)
    return (1.0 - surface_reflect * cosine) * scale, surface_reflect * sine * scale


def exchange_kernel(
    records,
    per_device,
    stride,
    traces,
    forward,
    wave_table,
    back_table,
    vertical_table,
    taps,
    inverse_table,
    depth,
    shot_slot,
    home,
    receiver,
    last,
    energy,
    summed,
    raw,
    rounded,
    table,
    wave,
    back,
    vertical,
    lag,
    inverse,
    placed,
    spectra,
    lifted,
    packed,
    shots,
    ordered,
    filtered,
    sums,
    load_sem,
    send_sem,
    recv_sem,
    sum_send,
    sum_recv,
    *slots,
):
    chunks = len(GROUPS)
    outgoing, arrived = slots[:chunks], slots[chunks:]
    me = lax.axis_index("shard")
    n_channels, n_samples = raw.shape
    padded = rounded.shape[0]
    half_rows = padded // 2
    home_rows = placed.shape[0]
    peers = records - 1
    firsts = [sum(GROUPS[:c]) for c in range(chunks + 1)]
    bounds = band_rows(per_device)
    finished = [bound // per_device for bound in bounds[:-1]] + [firsts[-1]]

    start = (lax.rem(me // 4, 2) * 2 + lax.rem(me, 2)) * peers // 4

    def turn(i):
        return peers - lax.rem(start + i, peers)

    def partner(step):
        if records & (records - 1):
            return lax.rem(me + step, records)
        other = 0
        bit = 1
        while bit < records:
            other = other + bit * lax.rem(me // bit + step // bit, 2)
            bit *= 2
        return other

    sem_count = [0]

    def load(source, target):
        copy = pltpu.make_async_copy(source, target, load_sem.at[sem_count[0]])
        sem_count[0] += 1
        copy.start()
        return copy

    def load_columns(c):
        lanes = pl.ds(firsts[c] * LANES, GROUPS[c] * LANES)
        return load(forward.at[:, lanes], table.at[:, lanes])

    piece = round_up(-(-padded // 3), 16)
    back_load = load(back_table, back)
    column_loads = [load_columns(0)]
    pieces = []
    for row in range(0, padded, piece):
        end = min(row + piece, n_channels)
        middle = row + round_up((end - row) // 2, 8)
        halves = [pl.ds(row, middle - row), pl.ds(middle, end - middle)]
        pieces.append((row, end, [load(traces.at[rows, :], raw.at[rows, :]) for rows in halves]))
    wave_load = load(wave_table, wave)
    near = pl.ds(0, firsts[1] * LANES)
    far = pl.ds(firsts[1] * LANES, (firsts[-1] - firsts[1]) * LANES)
    vertical_load = load(vertical_table.at[:, near], vertical.at[:, near])

    barrier = pltpu.get_barrier_semaphore()
    for step in range(1, records):
        pl.semaphore_signal(
            barrier,
            inc=1,
            device_id={"shard": partner(step)},
            device_id_type=pl.DeviceIdType.MESH,
        )

    packed[...] = jnp.zeros_like(packed)
    rounded[n_channels // 16 * 16 :, :] = jnp.zeros_like(rounded[n_channels // 16 * 16 :, :])
    n_bins = home.shape[0]
    homes = home[...].reshape(1, n_bins)
    moved = homes
    for d in range(1, records):
        moved = moved + jnp.where(homes >= d * per_device, stride - per_device, 0)
    bins = lax.broadcasted_iota(jnp.int32, (n_bins, n_channels), 0)
    chosen = (bins == receiver[...].reshape(1, n_channels)).astype(jnp.bfloat16)
    back_load.wait()
    by_bin = jnp.dot(chosen, back[...], preferred_element_type=jnp.float32).astype(jnp.bfloat16)
    rows = lax.broadcasted_iota(jnp.int32, (home_rows, n_bins), 0)
    chosen = (rows == moved).astype(jnp.bfloat16)
    placed[...] = jnp.dot(chosen, by_bin, preferred_element_type=jnp.float32).astype(jnp.bfloat16)

    def gains(c):
        return [
            gain_tiles(vertical[:, j * LANES : (j + 1) * LANES], depth[0], n_channels)
            for j in range(firsts[c], firsts[c + 1])
        ]

    vertical_load.wait()
    band_gains = gains(0)
    column_loads[0].wait()
    for row, end, copies in pieces:
        for copy in copies:
            copy.wait()
        rounded[row:end, :] = raw[row:end, :].astype(jnp.bfloat16)
        full = min(row + piece, padded)
        spectra[row:full, : GROUPS[0] * LANES] = jnp.dot(
            rounded[row:full, :],
            table[:, : GROUPS[0] * LANES],
            preferred_element_type=jnp.float32,
        ).astype(jnp.bfloat16)
    column_loads += [load_columns(c) for c in range(1, chunks)]
    far_load = load(vertical_table.at[:, far], vertical.at[:, far])
    lag_load = load(taps, lag)
    inverse_load = load(inverse_table, inverse)

    total = jnp.zeros((8, LANES), jnp.float32)
    sends = []
    for c, group in enumerate(GROUPS):
        if c == 0:
            wave_load.wait()
        else:
            column_loads[c].wait()
            if c == 1:
                far_load.wait()
            band_gains = gains(c)
            spectra[:, : group * LANES] = jnp.dot(
                rounded[...],
                table[:, firsts[c] * LANES : firsts[c + 1] * LANES],
                preferred_element_type=jnp.float32,
            ).astype(jnp.bfloat16)
        turned = jnp.dot(
            wave[...], spectra[:, : group * LANES], preferred_element_type=jnp.float32
        )
        for b, (straight, crossed) in enumerate(band_gains):
            lanes = slice(b * LANES, (b + 1) * LANES)
            for part in range(2):
                part_rows = slice(part * half_rows, (part + 1) * half_rows)
                value = turned[part_rows, lanes]
                lifted[part_rows, lanes] = (
                    straight * value + crossed * pltpu.roll(value, HALF, 1)
                ).astype(jnp.bfloat16)
        cleaned = jnp.dot(
            placed[...], lifted[:, : group * LANES], preferred_element_type=jnp.float32
        )
        for b in range(group):
            block = cleaned[:, b * LANES : (b + 1) * LANES]
            total = total + jnp.sum((block * block).reshape(-1, 8, LANES), axis=0)
            first = (firsts[c] + b) * per_device
            for d in range(records):
                packed[d, first : first + per_device, :] = block[
                    d * stride : d * stride + per_device
                ]
        outgoing[c][...] = packed[:, bounds[c] : bounds[c + 1], :].astype(jnp.bfloat16)
        if c == 0:
            pl.semaphore_wait(barrier, peers)
        for i in range(peers):
            step = turn(i)
            other = partner(step)
            send = pltpu.make_async_remote_copy(
                src_ref=outgoing[c].at[other],
                dst_ref=arrived[c].at[me],
                send_sem=send_sem.at[c, step - 1],
                recv_sem=recv_sem.at[c, step - 1],
                device_id={"shard": other},
                device_id_type=pl.DeviceIdType.MESH,
            )
            send.start()
            sends.append(send)
        arrived[c][me] = outgoing[c][me]

    sums[me] = total
    for i in range(peers):
        step = turn(i)
        send = pltpu.make_async_remote_copy(
            src_ref=sums.at[me],
            dst_ref=sums.at[me],
            send_sem=sum_send.at[step - 1],
            recv_sem=sum_recv.at[step - 1],
            device_id={"shard": partner(step)},
            device_id_type=pl.DeviceIdType.MESH,
        )
        send.start()
        sends.append(send)

    order = []
    for q in range(records):
        place = jnp.int32(0)
        for s in range(records):
            place = jnp.where(shot_slot[s] == q, s, place)
        order.append(place)
    lag_load.wait()
    inverse_load.wait()
    tile = 16
    done = 0
    for c, group in enumerate(GROUPS):
        for send in sends[c * peers : (c + 1) * peers]:
            send.wait()

        def filter_rows(r, carry):
            at = pl.ds(pl.multiple_of(r * tile, tile), tile)
            tap_at = pl.ds(pl.multiple_of(bounds[c] + r * tile, tile), tile)
            values = [arrived[c][order[q], at, :].astype(jnp.float32) for q in range(records)]
            for p in range(records):
                result = None
                for q in range(records):
                    term = lag[abs(p - q), tap_at, :] * values[q]
                    result = term if result is None else result + term
                shots[p, tap_at, :] = result
            return carry

        lax.fori_loop(0, (bounds[c + 1] - bounds[c]) // tile, filter_rows, 0)
        for j in range(finished[c], finished[c + 1]):
            for p in range(records):
                ordered[j, pl.ds(p, per_device, stride=records), :] = shots[
                    p, j * per_device : (j + 1) * per_device, :
                ]
            if c == chunks - 1:
                b = j - finished[c]
                last[:, b * LANES : (b + 1) * LANES] = ordered[j].astype(jnp.bfloat16)
            else:
                filtered[:, j * LANES : (j + 1) * LANES] = ordered[j].astype(jnp.bfloat16)
        if 0 < c < chunks - 1:
            depth_at = slice(done * LANES, finished[c + 1] * LANES)
            for n in range(0, n_samples, 512):
                part = jnp.dot(
                    filtered[:, depth_at],
                    inverse[depth_at, n : n + 512],
                    preferred_element_type=jnp.float32,
                )
                if done:
                    part = summed[:, n : n + 512] + part
                summed[:, n : n + 512] = part
            done = finished[c + 1]
    for send in sends[chunks * peers :]:
        send.wait()
    energy[...] = jnp.sum(sums[...], axis=0)


def exchange(traces, cable_depth, receiver, shot_slot, gather_home, tables, records):
    forward, inverse, wave, back, vertical, taps = tables
    back = back[: traces.shape[0]]
    n_channels, n_samples = traces.shape
    n_bins = gather_home.shape[0]
    per_device = n_bins // records
    stride = round_up(per_device, 16)
    padded = wave.shape[0]
    n_rows = per_device * records
    chunks = len(GROUPS)
    bounds = band_rows(per_device)
    late = sum(GROUPS) - bounds[-2] // per_device
    early = (sum(GROUPS) - late) * LANES
    vmem = pl.BlockSpec(memory_space=pltpu.VMEM)
    smem = pl.BlockSpec(memory_space=pltpu.SMEM)
    anywhere = pl.BlockSpec(memory_space=pl.ANY)
    width = max(GROUPS) * LANES
    packed = [bounds[c + 1] - bounds[c] for c in range(chunks)]
    peers = records - 1
    slots = [pltpu.VMEM((records, rows, LANES), jnp.bfloat16) for rows in packed]
    return pl.pallas_call(
        functools.partial(exchange_kernel, records, per_device, stride),
        out_shape=(
            pltpu.VMEM((n_rows, late * LANES), jnp.bfloat16),
            pltpu.VMEM((8, LANES), jnp.float32),
            pltpu.VMEM((n_rows, n_samples), jnp.float32),
        ),
        in_specs=[anywhere] * 7 + [smem, smem, vmem, vmem],
        out_specs=(vmem, vmem, vmem),
        scratch_shapes=[
            pltpu.VMEM((n_channels, n_samples), jnp.float32),
            pltpu.VMEM((padded, n_samples), jnp.bfloat16),
            pltpu.VMEM(forward.shape, jnp.bfloat16),
            pltpu.VMEM(wave.shape, jnp.bfloat16),
            pltpu.VMEM(back.shape, jnp.bfloat16),
            pltpu.VMEM(vertical.shape, jnp.float32),
            pltpu.VMEM(taps.shape, jnp.float32),
            pltpu.VMEM((early, n_samples), jnp.bfloat16),
            pltpu.VMEM((records * stride, padded), jnp.bfloat16),
            pltpu.VMEM((padded, width), jnp.bfloat16),
            pltpu.VMEM((padded, width), jnp.bfloat16),
            pltpu.VMEM((records, bounds[-1], LANES), jnp.float32),
            pltpu.VMEM((records, bounds[-1], LANES), jnp.float32),
            pltpu.VMEM((sum(GROUPS), n_rows, LANES), jnp.float32),
            pltpu.VMEM((n_rows, early), jnp.bfloat16),
            pltpu.VMEM((records, 8, LANES), jnp.float32),
            pltpu.SemaphoreType.DMA((24,)),
            pltpu.SemaphoreType.DMA((chunks, peers)),
            pltpu.SemaphoreType.DMA((chunks, peers)),
            pltpu.SemaphoreType.DMA((peers,)),
            pltpu.SemaphoreType.DMA((peers,)),
        ]
        + slots
        + slots,
        compiler_params=pltpu.CompilerParams(
            collective_id=0, has_side_effects=True, vmem_limit_bytes=54 * 1024 * 1024
        ),
    )(
        traces,
        forward,
        wave,
        back,
        vertical,
        taps,
        inverse[:early],
        cable_depth,
        shot_slot,
        gather_home,
        receiver,
    )


def inverse_kernel(count, block, energy, partial, filtered, inverse, out, staged, sems):
    total = jnp.sum(energy[...])
    scale = lax.rsqrt(jnp.full((1, 1), 2.0 * FREQ, jnp.float32) * (total / count + energy_eps))
    stores = []
    for i, row in enumerate(range(0, partial.shape[0], block)):
        rows = slice(row, row + block)
        staged[rows, :] = (
            partial[rows, :]
            + jnp.dot(filtered[rows, :], inverse[...], preferred_element_type=jnp.float32)
        ) * scale
        store = pltpu.make_async_copy(
            staged.at[pl.ds(row, block), :], out.at[pl.ds(row, block), :], sems.at[i]
        )
        store.start()
        stores.append(store)
    for store in stores:
        store.wait()


def invert(partial, filtered, energy, inverse, count):
    n_rows, n_samples = partial.shape
    depth = filtered.shape[1]
    block = max(rows for rows in range(16, 129, 16) if n_rows % rows == 0)
    vmem = pl.BlockSpec(memory_space=pltpu.VMEM)
    return pl.pallas_call(
        functools.partial(inverse_kernel, count, block),
        out_shape=jax.ShapeDtypeStruct((n_rows, n_samples), jnp.float32),
        in_specs=[vmem] * 4,
        out_specs=pl.BlockSpec(memory_space=pl.ANY),
        scratch_shapes=[
            pltpu.VMEM((n_rows, n_samples), jnp.float32),
            pltpu.SemaphoreType.DMA((n_rows // block,)),
        ],
        compiler_params=pltpu.CompilerParams(vmem_limit_bytes=40 * 1024 * 1024),
    )(energy, partial, filtered, inverse[-depth:])


def fused_shards(traces, cable_depth, receiver, shot_slot, gather_home):
    records = lax.axis_size("shard")
    n_channels, n_samples = traces.shape
    per_device = gather_home.shape[0] // records
    tables = fused_tables(n_channels, n_samples, records, per_device)
    last, energy, partial = exchange(
        traces, cable_depth, receiver, shot_slot, gather_home, tables, records
    )
    out = invert(partial, last, energy, tables[1], float(n_channels * records * FREQ))
    return out.reshape(per_device, records, n_samples)


def solution(mesh):
    in_specs = (
        P(("groups", "shard"), None),
        P(("groups", "shard")),
        P(("groups", "shard")),
        P("groups"),
        P("groups"),
    )
    out_specs = P(("groups", "shard"), None, None)
    body = fused_shards if mesh.shape["shard"] <= 16 else shards
    return jax.shard_map(body, mesh=mesh, in_specs=in_specs, out_specs=out_specs, check_vma=False)
```

```python
import functools
import math

import jax
import jax.numpy as jnp
import ml_dtypes
import numpy as np
from jax import lax
from jax.experimental import pallas as pl
from jax.experimental.pallas import tpu as pltpu
from jax.sharding import PartitionSpec as P

FREQ = 576


sample_step = 0.002
water_speed = 1500.0
channel_spacing = 12.5
shot_spacing = 25.0
surface_reflect = 0.9
ghost_floor = 0.1
reject_speed = 1500.0
low_floor = 4.0 * math.pi
energy_eps = 1e-06


def forward_time(n_samples, first_bin, band_size):
    samples = jnp.arange(n_samples, dtype=jnp.int32)
    freq_bins = first_bin + jnp.arange(band_size, dtype=jnp.int32)
    angles = (samples[:, None] * freq_bins[None, :] % n_samples).astype(jnp.float32) * (
        2.0 * math.pi / n_samples
    )
    return jnp.concatenate([jnp.cos(angles), -jnp.sin(angles)], axis=1).astype(jnp.bfloat16)


def inverse_time(n_samples, first_bin, band_size):
    samples = jnp.arange(n_samples, dtype=jnp.int32)
    freq_bins = first_bin + jnp.arange(band_size, dtype=jnp.int32)
    angles = (freq_bins[:, None] * samples[None, :] % n_samples).astype(jnp.float32) * (
        2.0 * math.pi / n_samples
    )
    weights = jnp.where(freq_bins == 0, 1.0, 2.0).astype(jnp.float32)[:, None]
    return jnp.concatenate([weights * jnp.cos(angles), -weights * jnp.sin(angles)], axis=0).astype(
        jnp.bfloat16
    )


def wave_tables(n_channels):
    wave_index = jnp.arange(n_channels, dtype=jnp.int32)
    angles = (wave_index[:, None] * wave_index[None, :] % n_channels).astype(jnp.float32) * (
        2.0 * math.pi / n_channels
    )
    return (jnp.cos(angles).astype(jnp.bfloat16), jnp.sin(angles).astype(jnp.bfloat16))


def angular_band(n_samples, first_bin, band_size):
    freq_bins = (first_bin + jnp.arange(band_size, dtype=jnp.int32)).astype(jnp.float32)
    return 2.0 * math.pi * freq_bins / (n_samples * sample_step)


def ghost_operator(n_channels, n_samples, first_bin, band_size, depth_value):
    angular = angular_band(n_samples, first_bin, band_size)
    wave_index = jnp.arange(n_channels, dtype=jnp.int32)
    signed = jnp.where(wave_index <= n_channels // 2, wave_index, wave_index - n_channels).astype(
        jnp.float32
    )
    wave_number = 2.0 * math.pi * signed / (n_channels * channel_spacing)
    slowness = angular / water_speed
    vertical = jnp.sqrt(
        jnp.maximum(
            slowness[None, :] * slowness[None, :] - wave_number[:, None] * wave_number[:, None], 0.0
        )
    )
    angles = 2.0 * vertical * depth_value
    cosine = jnp.cos(angles)
    denominator = (
        1.0 - 2.0 * surface_reflect * cosine + surface_reflect * surface_reflect + ghost_floor
    )
    return (
        (1.0 - surface_reflect * cosine) / denominator,
        -surface_reflect * jnp.sin(angles) / denominator,
    )


def deghost(record, depth_value, first_bin, band_size):
    n_channels, n_samples = record.shape
    spectra = jnp.dot(
        record.astype(jnp.bfloat16),
        forward_time(n_samples, first_bin, band_size),
        preferred_element_type=jnp.float32,
    ).astype(jnp.bfloat16)
    cos_wave, sin_wave = wave_tables(n_channels)
    plain = jnp.dot(cos_wave, spectra, preferred_element_type=jnp.float32)
    turned = jnp.dot(sin_wave, spectra, preferred_element_type=jnp.float32)
    wave_re = plain[:, :band_size] + turned[:, band_size:]
    wave_im = plain[:, band_size:] - turned[:, :band_size]
    gain_re, gain_im = ghost_operator(n_channels, n_samples, first_bin, band_size, depth_value)
    lifted = jnp.concatenate(
        [gain_re * wave_re - gain_im * wave_im, gain_re * wave_im + gain_im * wave_re], axis=1
    ).astype(jnp.bfloat16)
    plain = jnp.dot(cos_wave, lifted, preferred_element_type=jnp.float32)
    turned = jnp.dot(sin_wave, lifted, preferred_element_type=jnp.float32)
    back_re = (plain[:, :band_size] - turned[:, band_size:]) / n_channels
    back_im = (plain[:, band_size:] + turned[:, :band_size]) / n_channels
    cleaned = jnp.concatenate([back_re, back_im], axis=1)
    return (cleaned.astype(jnp.bfloat16), jnp.sum(cleaned * cleaned))


def shot_tables(positions, records):
    wave_index = jnp.arange(2 * records, dtype=jnp.int32)
    angles = (positions[:, None] * wave_index[None, :] % (2 * records)).astype(jnp.float32) * (
        math.pi / records
    )
    return (jnp.cos(angles).astype(jnp.bfloat16), jnp.sin(angles).astype(jnp.bfloat16))


def shot_filter(records, n_samples, first_bin, band_size):
    angular = angular_band(n_samples, first_bin, band_size)
    wave_index = jnp.arange(2 * records, dtype=jnp.int32)
    signed = jnp.where(wave_index <= records, wave_index, wave_index - 2 * records).astype(
        jnp.float32
    )
    shot_number = 2.0 * math.pi * signed / (2 * records * shot_spacing)
    reject_ratio = reject_speed * jnp.abs(shot_number)[:, None] / (angular[None, :] + low_floor)
    squared = reject_ratio * reject_ratio
    response = 1.0 / (1.0 + squared * squared) / (2.0 * records)
    return jnp.concatenate([response, response], axis=1)


def place_rows(clean_rows, receiver, gather_home, records, per_device):
    targets = jnp.take(gather_home, receiver, axis=0)
    buffer = (
        jnp.zeros((records * per_device, clean_rows.shape[1]), jnp.bfloat16)
        .at[targets]
        .set(clean_rows)
    )
    return buffer.reshape(records, per_device, clean_rows.shape[1])


def filter_gathers(arrived, shot_slot, n_samples, first_bin, band_size):
    records = arrived.shape[0]
    cos_source, sin_source = shot_tables(shot_slot, records)
    cos_shot, sin_shot = shot_tables(jnp.arange(records, dtype=jnp.int32), records)
    response = shot_filter(records, n_samples, first_bin, band_size)[:, None, :]
    even_part = (
        jnp.einsum("sgf,sk->kgf", arrived, cos_source, preferred_element_type=jnp.float32)
        * response
    ).astype(jnp.bfloat16)
    odd_part = (
        jnp.einsum("sgf,sk->kgf", arrived, sin_source, preferred_element_type=jnp.float32)
        * response
    ).astype(jnp.bfloat16)
    filtered = (
        jnp.einsum("pk,kgf->gpf", cos_shot, even_part, preferred_element_type=jnp.float32)
        + jnp.einsum("pk,kgf->gpf", sin_shot, odd_part, preferred_element_type=jnp.float32)
    ).astype(jnp.bfloat16)
    return jnp.einsum(
        "gpf,ft->gpt",
        filtered,
        inverse_time(n_samples, first_bin, band_size),
        preferred_element_type=jnp.float32,
    )


def shards(traces, cable_depth, receiver, shot_slot, gather_home):
    records = lax.axis_size("shard")
    per_device = gather_home.shape[0] // records
    n_channels, n_samples = traces.shape
    clean_rows, energy = deghost(traces, cable_depth[0], 0, FREQ)
    outgoing = place_rows(clean_rows, receiver, gather_home, records, per_device)
    arrived = lax.all_to_all(outgoing, "shard", split_axis=0, concat_axis=0, tiled=True)
    summed = filter_gathers(arrived, shot_slot, n_samples, 0, FREQ)
    total_energy = lax.psum(energy, "shard")
    out_scale = 1.0 / jnp.sqrt(
        2.0 * FREQ * (total_energy / (n_channels * records * FREQ) + energy_eps)
    )
    return summed * out_scale


def round_up(value, unit):
    return -(-value // unit) * unit


LANES = 128
HALF = LANES // 2
GROUPS = (2, 2, 2, 2, 1)


def band_rows(per_device):
    ends = [sum(GROUPS[: c + 1]) * per_device for c in range(len(GROUPS))]
    return [0] + [end // 16 * 16 for end in ends[:-1]] + [round_up(ends[-1], 16)]


def fused_tables(n_channels, n_samples, records, per_device):
    bf16 = ml_dtypes.bfloat16
    blocks = FREQ // HALF
    bins = np.arange(FREQ).reshape(blocks, HALF)
    samples = np.arange(n_samples)
    turn = 2.0 * np.pi / n_samples
    angle = (samples[:, None] * np.arange(FREQ)[None, :] % n_samples) * turn
    cos_t = np.cos(angle).reshape(n_samples, blocks, 1, HALF)
    sin_t = np.sin(angle).reshape(n_samples, blocks, 1, HALF)
    forward = np.concatenate([cos_t, -sin_t], axis=2).reshape(n_samples, blocks * LANES)
    weight = np.where(bins == 0, 1.0, 2.0)[None, :, None, :]
    inverse = np.concatenate([weight * cos_t, -weight * sin_t], axis=2)
    inverse = inverse.reshape(n_samples, blocks * LANES).T
    half_rows = round_up(n_channels // 2 + 1, 16)
    wave = np.zeros((2 * half_rows, 2 * half_rows))
    index = np.arange(n_channels // 2 + 1)
    angle = (index[:, None] * np.arange(n_channels)[None, :] % n_channels) * (
        2.0 * np.pi / n_channels
    )
    wave[: index.size, :n_channels] = np.cos(angle)
    wave[half_rows : half_rows + index.size, :n_channels] = np.sin(angle)
    own_mirror = (index * 2) % n_channels == 0
    wave[half_rows : half_rows + index.size][own_mirror] = 0.0
    twice = np.ones((2 * half_rows, 1))
    twice[: index.size, 0] = np.where(own_mirror, 1.0, 2.0)
    twice[half_rows : half_rows + index.size, 0] = 2.0
    wave = wave.astype(bf16)
    back = (wave.astype(np.float64) * twice).T.astype(bf16)

    angular = 2.0 * np.pi * np.arange(FREQ) / (n_samples * sample_step)
    number = 2.0 * np.pi * np.arange(half_rows) / (n_channels * channel_spacing)
    vertical = np.sqrt(
        np.maximum((angular / water_speed)[None, :] ** 2 - number[:, None] ** 2, 0.0)
    )
    vertical = (vertical / np.pi).reshape(half_rows, blocks, 1, HALF)
    vertical = np.concatenate([vertical, vertical], axis=2).reshape(half_rows, blocks * LANES)

    shots = np.arange(2 * records)
    signed = np.where(shots <= records, shots, shots - 2 * records)
    shot_number = 2.0 * np.pi * signed / (2 * records * shot_spacing)
    ratio = reject_speed * np.abs(shot_number)[:, None] / (angular[None, :] + low_floor)
    response = 1.0 / (1.0 + ratio**4) / (2.0 * records)
    apart = np.arange(records)
    lag = np.cos(np.pi / records * (apart[:, None] * shots[None, :] % (2 * records))) @ response
    lag = lag.reshape(records, blocks, 1, HALF)
    lag = np.concatenate([lag, lag], axis=2).reshape(records, blocks, 1, LANES)
    lag = np.broadcast_to(lag, (records, blocks, per_device, LANES))
    taps = np.zeros((records, band_rows(per_device)[-1], LANES))
    taps[:, : blocks * per_device] = lag.reshape(records, blocks * per_device, LANES)
    return (
        forward.astype(bf16),
        inverse.astype(bf16),
        wave,
        back,
        vertical.astype(np.float32),
        taps.astype(np.float32),
    )


SINE = [(-1.0) ** i * (2.0 * math.pi) ** (2 * i + 1) / math.factorial(2 * i + 1) for i in range(6)]


def gain_tiles(vertical, depth, n_channels):
    left = lax.broadcasted_iota(jnp.int32, vertical.shape, 1) < HALF
    turns = vertical * depth - jnp.where(left, 0.25, 0.0)
    offset = 0.25 - jnp.abs(turns - jnp.floor(turns + 0.5))
    square = offset * offset
    value = jnp.full_like(square, SINE[-1])
    for coefficient in SINE[-2::-1]:
        value = value * square + coefficient
    value = value * offset
    swapped = pltpu.roll(value, HALF, 1)
    cosine = jnp.where(left, swapped, value)
    sine = jnp.where(left, value, -swapped)
    denominator = (
        1.0 - 2.0 * surface_reflect * cosine + surface_reflect * surface_reflect + ghost_floor
    )
    scale = 1.0 / (denominator * n_channels)
    return (1.0 - surface_reflect * cosine) * scale, surface_reflect * sine * scale


def exchange_kernel(
    records,
    per_device,
    stride,
    traces,
    forward,
    wave_table,
    back_table,
    vertical_table,
    taps,
    inverse_table,
    depth,
    shot_slot,
    home,
    receiver,
    last,
    energy,
    summed,
    raw,
    rounded,
    table,
    wave,
    back,
    vertical,
    lag,
    inverse,
    placed,
    spectra,
    lifted,
    packed,
    shots,
    ordered,
    filtered,
    sums,
    load_sem,
    send_sem,
    recv_sem,
    sum_send,
    sum_recv,
    *slots,
):
    chunks = len(GROUPS)
    outgoing, arrived = slots[:chunks], slots[chunks:]
    me = lax.axis_index("shard")
    n_channels, n_samples = raw.shape
    padded = rounded.shape[0]
    half_rows = padded // 2
    home_rows = placed.shape[0]
    peers = records - 1
    firsts = [sum(GROUPS[:c]) for c in range(chunks + 1)]
    bounds = band_rows(per_device)
    finished = [bound // per_device for bound in bounds[:-1]] + [firsts[-1]]

    start = (lax.rem(me // 4, 2) * 2 + lax.rem(me, 2)) * peers // 4

    def turn(i):
        return peers - lax.rem(start + i, peers)

    def partner(step):
        if records & (records - 1):
            return lax.rem(me + step, records)
        other = 0
        bit = 1
        while bit < records:
            other = other + bit * lax.rem(me // bit + step // bit, 2)
            bit *= 2
        return other

    sem_count = [0]

    def load(source, target):
        copy = pltpu.make_async_copy(source, target, load_sem.at[sem_count[0]])
        sem_count[0] += 1
        copy.start()
        return copy

    def load_columns(c):
        lanes = pl.ds(firsts[c] * LANES, GROUPS[c] * LANES)
        return load(forward.at[:, lanes], table.at[:, lanes])

    piece = round_up(-(-padded // 3), 16)
    back_load = load(back_table, back)
    column_loads = [load_columns(0)]
    pieces = []
    for row in range(0, padded, piece):
        end = min(row + piece, n_channels)
        middle = row + round_up((end - row) // 2, 8)
        halves = [pl.ds(row, middle - row), pl.ds(middle, end - middle)]
        pieces.append((row, end, [load(traces.at[rows, :], raw.at[rows, :]) for rows in halves]))
    wave_load = load(wave_table, wave)
    near = pl.ds(0, firsts[1] * LANES)
    far = pl.ds(firsts[1] * LANES, (firsts[-1] - firsts[1]) * LANES)
    vertical_load = load(vertical_table.at[:, near], vertical.at[:, near])

    barrier = pltpu.get_barrier_semaphore()
    for step in range(1, records):
        pl.semaphore_signal(
            barrier,
            inc=1,
            device_id={"shard": partner(step)},
            device_id_type=pl.DeviceIdType.MESH,
        )

    packed[...] = jnp.zeros_like(packed)
    rounded[n_channels // 16 * 16 :, :] = jnp.zeros_like(rounded[n_channels // 16 * 16 :, :])
    n_bins = home.shape[0]
    homes = home[...].reshape(1, n_bins)
    moved = homes
    for d in range(1, records):
        moved = moved + jnp.where(homes >= d * per_device, stride - per_device, 0)
    bins = lax.broadcasted_iota(jnp.int32, (n_bins, n_channels), 0)
    chosen = (bins == receiver[...].reshape(1, n_channels)).astype(jnp.bfloat16)
    back_load.wait()
    by_bin = jnp.dot(chosen, back[...], preferred_element_type=jnp.float32).astype(jnp.bfloat16)
    rows = lax.broadcasted_iota(jnp.int32, (home_rows, n_bins), 0)
    chosen = (rows == moved).astype(jnp.bfloat16)
    placed[...] = jnp.dot(chosen, by_bin, preferred_element_type=jnp.float32).astype(jnp.bfloat16)

    def gains(c):
        return [
            gain_tiles(vertical[:, j * LANES : (j + 1) * LANES], depth[0], n_channels)
            for j in range(firsts[c], firsts[c + 1])
        ]

    vertical_load.wait()
    band_gains = gains(0)
    column_loads[0].wait()
    for row, end, copies in pieces:
        for copy in copies:
            copy.wait()
        rounded[row:end, :] = raw[row:end, :].astype(jnp.bfloat16)
        full = min(row + piece, padded)
        spectra[row:full, : GROUPS[0] * LANES] = jnp.dot(
            rounded[row:full, :],
            table[:, : GROUPS[0] * LANES],
            preferred_element_type=jnp.float32,
        ).astype(jnp.bfloat16)
    column_loads += [load_columns(c) for c in range(1, chunks)]
    far_load = load(vertical_table.at[:, far], vertical.at[:, far])
    lag_load = load(taps, lag)
    inverse_load = load(inverse_table, inverse)

    total = jnp.zeros((8, LANES), jnp.float32)
    sends = []
    for c, group in enumerate(GROUPS):
        if c == 0:
            wave_load.wait()
        else:
            column_loads[c].wait()
            if c == 1:
                far_load.wait()
            band_gains = gains(c)
            spectra[:, : group * LANES] = jnp.dot(
                rounded[...],
                table[:, firsts[c] * LANES : firsts[c + 1] * LANES],
                preferred_element_type=jnp.float32,
            ).astype(jnp.bfloat16)
        turned = jnp.dot(
            wave[...], spectra[:, : group * LANES], preferred_element_type=jnp.float32
        )
        for b, (straight, crossed) in enumerate(band_gains):
            lanes = slice(b * LANES, (b + 1) * LANES)
            for part in range(2):
                part_rows = slice(part * half_rows, (part + 1) * half_rows)
                value = turned[part_rows, lanes]
                lifted[part_rows, lanes] = (
                    straight * value + crossed * pltpu.roll(value, HALF, 1)
                ).astype(jnp.bfloat16)
        cleaned = jnp.dot(
            placed[...], lifted[:, : group * LANES], preferred_element_type=jnp.float32
        )
        for b in range(group):
            block = cleaned[:, b * LANES : (b + 1) * LANES]
            total = total + jnp.sum((block * block).reshape(-1, 8, LANES), axis=0)
            first = (firsts[c] + b) * per_device
            for d in range(records):
                packed[d, first : first + per_device, :] = block[
                    d * stride : d * stride + per_device
                ]
        outgoing[c][...] = packed[:, bounds[c] : bounds[c + 1], :].astype(jnp.bfloat16)
        if c == 0:
            pl.semaphore_wait(barrier, peers)
        for i in range(peers):
            step = turn(i)
            other = partner(step)
            send = pltpu.make_async_remote_copy(
                src_ref=outgoing[c].at[other],
                dst_ref=arrived[c].at[me],
                send_sem=send_sem.at[c, step - 1],
                recv_sem=recv_sem.at[c, step - 1],
                device_id={"shard": other},
                device_id_type=pl.DeviceIdType.MESH,
            )
            send.start()
            sends.append(send)
        arrived[c][me] = outgoing[c][me]

    sums[me] = total
    for i in range(peers):
        step = turn(i)
        send = pltpu.make_async_remote_copy(
            src_ref=sums.at[me],
            dst_ref=sums.at[me],
            send_sem=sum_send.at[step - 1],
            recv_sem=sum_recv.at[step - 1],
            device_id={"shard": partner(step)},
            device_id_type=pl.DeviceIdType.MESH,
        )
        send.start()
        sends.append(send)

    order = []
    for q in range(records):
        place = jnp.int32(0)
        for s in range(records):
            place = jnp.where(shot_slot[s] == q, s, place)
        order.append(place)
    lag_load.wait()
    inverse_load.wait()
    tile = 16
    done = 0
    for c, group in enumerate(GROUPS):
        for send in sends[c * peers : (c + 1) * peers]:
            send.wait()

        def filter_rows(r, carry):
            at = pl.ds(pl.multiple_of(r * tile, tile), tile)
            values = [arrived[c][order[q], at, :].astype(jnp.float32) for q in range(records)]
            for low in range(0, tile, 8):
                tap_at = pl.ds(pl.multiple_of(bounds[c] + r * tile + low, 8), 8)
                band_taps = [lag[apart, tap_at, :] for apart in range(records)]
                parts = [value[low : low + 8] for value in values]
                for p in range(records):
                    result = band_taps[p] * parts[0]
                    for q in range(1, records):
                        result = result + band_taps[abs(p - q)] * parts[q]
                    shots[p, tap_at, :] = result
            return carry

        lax.fori_loop(0, (bounds[c + 1] - bounds[c]) // tile, filter_rows, 0)
        for j in range(finished[c], finished[c + 1]):
            for p in range(records):
                ordered[j, pl.ds(p, per_device, stride=records), :] = shots[
                    p, j * per_device : (j + 1) * per_device, :
                ]
            if c == chunks - 1:
                b = j - finished[c]
                last[:, b * LANES : (b + 1) * LANES] = ordered[j].astype(jnp.bfloat16)
            else:
                filtered[:, j * LANES : (j + 1) * LANES] = ordered[j].astype(jnp.bfloat16)
        if 0 < c < chunks - 1:
            depth_at = slice(done * LANES, finished[c + 1] * LANES)
            for n in range(0, n_samples, 512):
                part = jnp.dot(
                    filtered[:, depth_at],
                    inverse[depth_at, n : n + 512],
                    preferred_element_type=jnp.float32,
                )
                if done:
                    part = summed[:, n : n + 512] + part
                summed[:, n : n + 512] = part
            done = finished[c + 1]
    for send in sends[chunks * peers :]:
        send.wait()
    energy[...] = jnp.sum(sums[...], axis=0)


def exchange(traces, cable_depth, receiver, shot_slot, gather_home, tables, records):
    forward, inverse, wave, back, vertical, taps = tables
    back = back[: traces.shape[0]]
    n_channels, n_samples = traces.shape
    n_bins = gather_home.shape[0]
    per_device = n_bins // records
    stride = round_up(per_device, 16)
    padded = wave.shape[0]
    n_rows = per_device * records
    chunks = len(GROUPS)
    bounds = band_rows(per_device)
    late = sum(GROUPS) - bounds[-2] // per_device
    early = (sum(GROUPS) - late) * LANES
    vmem = pl.BlockSpec(memory_space=pltpu.VMEM)
    smem = pl.BlockSpec(memory_space=pltpu.SMEM)
    anywhere = pl.BlockSpec(memory_space=pl.ANY)
    width = max(GROUPS) * LANES
    packed = [bounds[c + 1] - bounds[c] for c in range(chunks)]
    peers = records - 1
    slots = [pltpu.VMEM((records, rows, LANES), jnp.bfloat16) for rows in packed]
    return pl.pallas_call(
        functools.partial(exchange_kernel, records, per_device, stride),
        out_shape=(
            pltpu.VMEM((n_rows, late * LANES), jnp.bfloat16),
            pltpu.VMEM((8, LANES), jnp.float32),
            pltpu.VMEM((n_rows, n_samples), jnp.float32),
        ),
        in_specs=[anywhere] * 7 + [smem, smem, vmem, vmem],
        out_specs=(vmem, vmem, vmem),
        scratch_shapes=[
            pltpu.VMEM((n_channels, n_samples), jnp.float32),
            pltpu.VMEM((padded, n_samples), jnp.bfloat16),
            pltpu.VMEM(forward.shape, jnp.bfloat16),
            pltpu.VMEM(wave.shape, jnp.bfloat16),
            pltpu.VMEM(back.shape, jnp.bfloat16),
            pltpu.VMEM(vertical.shape, jnp.float32),
            pltpu.VMEM(taps.shape, jnp.float32),
            pltpu.VMEM((early, n_samples), jnp.bfloat16),
            pltpu.VMEM((records * stride, padded), jnp.bfloat16),
            pltpu.VMEM((padded, width), jnp.bfloat16),
            pltpu.VMEM((padded, width), jnp.bfloat16),
            pltpu.VMEM((records, bounds[-1], LANES), jnp.float32),
            pltpu.VMEM((records, bounds[-1], LANES), jnp.float32),
            pltpu.VMEM((sum(GROUPS), n_rows, LANES), jnp.float32),
            pltpu.VMEM((n_rows, early), jnp.bfloat16),
            pltpu.VMEM((records, 8, LANES), jnp.float32),
            pltpu.SemaphoreType.DMA((24,)),
            pltpu.SemaphoreType.DMA((chunks, peers)),
            pltpu.SemaphoreType.DMA((chunks, peers)),
            pltpu.SemaphoreType.DMA((peers,)),
            pltpu.SemaphoreType.DMA((peers,)),
        ]
        + slots
        + slots,
        compiler_params=pltpu.CompilerParams(
            collective_id=0, has_side_effects=True, vmem_limit_bytes=54 * 1024 * 1024
        ),
    )(
        traces,
        forward,
        wave,
        back,
        vertical,
        taps,
        inverse[:early],
        cable_depth,
        shot_slot,
        gather_home,
        receiver,
    )


def inverse_kernel(count, block, energy, partial, filtered, inverse, out, staged, sems):
    total = jnp.sum(energy[...])
    scale = lax.rsqrt(jnp.full((1, 1), 2.0 * FREQ, jnp.float32) * (total / count + energy_eps))
    stores = []
    for i, row in enumerate(range(0, partial.shape[0], block)):
        rows = slice(row, row + block)
        staged[rows, :] = (
            partial[rows, :]
            + jnp.dot(filtered[rows, :], inverse[...], preferred_element_type=jnp.float32)
        ) * scale
        store = pltpu.make_async_copy(
            staged.at[pl.ds(row, block), :], out.at[pl.ds(row, block), :], sems.at[i]
        )
        store.start()
        stores.append(store)
    for store in stores:
        store.wait()


def invert(partial, filtered, energy, inverse, count):
    n_rows, n_samples = partial.shape
    depth = filtered.shape[1]
    block = max(rows for rows in range(16, 129, 16) if n_rows % rows == 0)
    vmem = pl.BlockSpec(memory_space=pltpu.VMEM)
    return pl.pallas_call(
        functools.partial(inverse_kernel, count, block),
        out_shape=jax.ShapeDtypeStruct((n_rows, n_samples), jnp.float32),
        in_specs=[vmem] * 4,
        out_specs=pl.BlockSpec(memory_space=pl.ANY),
        scratch_shapes=[
            pltpu.VMEM((n_rows, n_samples), jnp.float32),
            pltpu.SemaphoreType.DMA((n_rows // block,)),
        ],
        compiler_params=pltpu.CompilerParams(vmem_limit_bytes=40 * 1024 * 1024),
    )(energy, partial, filtered, inverse[-depth:])


def fused_shards(traces, cable_depth, receiver, shot_slot, gather_home):
    records = lax.axis_size("shard")
    n_channels, n_samples = traces.shape
    per_device = gather_home.shape[0] // records
    tables = fused_tables(n_channels, n_samples, records, per_device)
    last, energy, partial = exchange(
        traces, cable_depth, receiver, shot_slot, gather_home, tables, records
    )
    out = invert(partial, last, energy, tables[1], float(n_channels * records * FREQ))
    return out.reshape(per_device, records, n_samples)


def solution(mesh):
    in_specs = (
        P(("groups", "shard"), None),
        P(("groups", "shard")),
        P(("groups", "shard")),
        P("groups"),
        P("groups"),
    )
    out_specs = P(("groups", "shard"), None, None)
    body = fused_shards if mesh.shape["shard"] <= 16 else shards
    return jax.shard_map(body, mesh=mesh, in_specs=in_specs, out_specs=out_specs, check_vma=False)
```
